1024 devices in a mesh: blk: 16 (over z, y_hi), group: 64 (over y_lo, x, core).
Axes of the slice: x: 8, y: 8 (y_hi: 2, y_lo: 4; y = y_hi * 4 + y_lo), z: 8, core: 2. Of those that a mesh axis runs over, the one named last changes fastest.
Arguments:
- images: bfloat16 [131072, 1152], P(('blk', 'group')), may hold values from -6 to 6
- texts: bfloat16 [131072, 1152], P(('blk', 'group')), may hold values from -6 to 6
- labels: int32 [16, 8192], P(None, 'group'), may hold values from 0 to 511
- weights: float32 [131072], P(('blk', 'group')), may hold values from 0.3 to 20
- log_temp: float32 [1], replicated, may hold values from 1.6 to 3
- bias: float32 [1], replicated, may hold values from -4 to -1
Outputs:
- image_grad: bfloat16 [131072, 1152], P(('blk', 'group'))
- text_grad: bfloat16 [131072, 1152], P(('blk', 'group'))
- stats: float32 [3], replicated
The draws below stay inside these ranges and needn't reach their ends.
All inputs are finite; a program needn't handle non-finite values.
Results may differ from the reference program's by a relative error of at most 0.0061.
Values may be sent and summed in bfloat16 or wider, within the bound.
No kernel may reach another device: no remote copies, remote signals or barrier semaphores. Data moves between devices by JAX's collectives and lax.ppermute only.
A program may use at most 32 MiB of HBM per device.

```python
import jax
import jax.numpy as jnp
from jax import lax

E = 1152
ROWS = 128
TOKENS = 131072
GROUP_ROWS = 8192
LABELS = 512
N_BLK = 16
N_GROUP = 64


def draw_weights(key, part):
    key = jax.random.fold_in(key, 7)
    blocks = max(TOKENS // ROWS - 1, 1)
    device_pos = (jnp.arange(TOKENS) // ROWS).astype(jnp.float32) / float(blocks)
    base = jnp.exp(jax.random.uniform(key, (TOKENS,), jnp.float32, jnp.log(0.5), jnp.log(2.0)))
    ramp = jnp.exp(device_pos * jnp.log(10.0))
    return (base * ramp).astype(jnp.float32)


def plant(array, rng, smallest, top_value):
    extent = array.shape
    place = [jax.random.randint(jax.random.fold_in(rng, axis), (), 0, extent[axis]) for axis in range(len(extent))]
    array = array.at[tuple(place)].set(smallest)
    longest = extent.index(max(extent))
    place[longest] = (place[longest] + 1) % extent[longest]
    return array.at[tuple(place)].set(top_value)


def shard_levels(own_key, dims, pieces, least, top_value):
    loudness, own = 1.0, jax.random.fold_in(own_key, 6)
    for axis_at, shards_of in pieces:
        steps = jnp.exp(jax.random.uniform(jax.random.fold_in(own, axis_at), (shards_of,), jnp.float32, least / len(pieces), top_value / len(pieces)))
        loudness = loudness * jnp.repeat(steps, dims[axis_at] // shards_of).reshape([-1 if axis == axis_at else 1 for axis in range(len(dims))])
    return loudness


def scatter_about(key, shape, spread, reach, cuts=(), dtype=jnp.bfloat16):
    result = spread * jax.random.normal(key, shape, jnp.float32)
    if cuts:
        result = result * shard_levels(key, shape, cuts, -0.22, 0.18)
    return jnp.clip(result, -reach, reach).astype(dtype)


def setup_inputs(seed: int = 0) -> dict:
    key_of = jax.random.split(jax.random.key(seed), 7)
    return {
        "images": scatter_about(key_of[0], (TOKENS, E), 1.0, 6.0, ((0, 1024),)),
        "texts": scatter_about(key_of[1], (TOKENS, E), 1.0, 6.0, ((0, 1024),)),
        "labels": plant(jax.random.randint(key_of[2], (N_BLK, GROUP_ROWS), 0, LABELS), jax.random.fold_in(key_of[2], 1), 0, LABELS - 1).astype(jnp.int32),
        "weights": draw_weights(jax.random.fold_in(key_of[6], 71), 0),
        "log_temp": jnp.clip(jax.random.uniform(key_of[4], (1,), jnp.float32, 1.6, 3.0), 1.6, 3.0),
        "bias": jnp.clip(jax.random.uniform(key_of[5], (1,), jnp.float32, -4.0, -1.0), -4.0, -1.0),
    }


def normalize(raw):
    values = raw.astype(jnp.float32)
    scale = lax.rsqrt(lax.optimization_barrier(jnp.sum(values * values, axis=-1, keepdims=True)) + 1e-06)
    return (values * scale, scale)

def norm_back(unit, scale, upstream):
    return (upstream - unit * lax.optimization_barrier(jnp.sum(unit * upstream, axis=-1, keepdims=True))) * scale

def reference(images, texts, labels, weights, log_temp, bias):
    cycle = N_BLK
    groups = N_GROUP
    span = min(8, cycle)
    half = span // 2
    image_norm, image_scale = normalize(images.reshape(cycle, groups, ROWS, E))
    text_norm, text_scale = normalize(texts.reshape(cycle, groups, ROWS, E))
    image_unit = image_norm.astype(jnp.bfloat16).astype(jnp.float32)
    text_unit = text_norm.astype(jnp.bfloat16).astype(jnp.float32)
    label_grid = labels.reshape(cycle, groups, ROWS)
    weight_grid = weights.reshape(cycle, groups, ROWS)
    temper = jnp.exp(log_temp[0])
    offset_bias = bias[0]
    image_total = jnp.zeros((cycle, groups, ROWS, E), jnp.float32)
    text_total = jnp.zeros((cycle, groups, ROWS, E), jnp.float32)
    sums = jnp.zeros((3,), jnp.float32)
    for offset in range(-(half - 1), half + 1):
        shifted = jnp.roll(text_unit, -offset, axis=0)
        shifted_label = jnp.roll(label_grid, -offset, axis=0)
        scores = jnp.einsum('bgie,bgje->bgij', image_unit, shifted, precision=lax.Precision.HIGHEST)
        scaled = temper * scores
        logits = scaled + offset_bias
        target = (label_grid[..., :, None] == shifted_label[..., None, :]).astype(jnp.float32)
        signed = 2.0 * target - 1.0
        grads = weight_grid[..., :, None] * (jax.nn.sigmoid(logits) - target)
        losses = weight_grid[..., :, None] * jax.nn.softplus(-signed * logits)
        rounded = grads.astype(jnp.bfloat16).astype(jnp.float32)
        image_total = image_total + temper * jnp.einsum('bgij,bgje->bgie', rounded, shifted, precision=lax.Precision.HIGHEST)
        text_part = temper * jnp.einsum('bgij,bgie->bgje', rounded, image_unit, precision=lax.Precision.HIGHEST)
        text_total = text_total + jnp.roll(text_part, offset, axis=0)
        sums = sums + jnp.stack([jnp.sum(losses), jnp.sum(grads * scaled), jnp.sum(grads)])
    image_grad = norm_back(image_norm, image_scale, image_total).astype(jnp.bfloat16).reshape(TOKENS, E)
    text_grad = norm_back(text_norm, text_scale, text_total).astype(jnp.bfloat16).reshape(TOKENS, E)
    count = float(TOKENS) * float(ROWS) * float(span)
    return (image_grad, text_grad, sums / count)
```

```python
import functools

import jax
import jax.numpy as jnp
from jax import lax
from jax.experimental import pallas as pl
from jax.experimental.pallas import tpu as pltpu
from jax.sharding import PartitionSpec as P

VMEM = pl.BlockSpec(memory_space=pltpu.VMEM)
SMEM = pl.BlockSpec(memory_space=pltpu.SMEM)
F32 = jnp.float32
BF16 = jnp.bfloat16
PARAMS = pltpu.CompilerParams(vmem_limit_bytes=40 * 1024 * 1024)


def shape(rows, cols, dtype):
    return jax.ShapeDtypeStruct((rows, cols), dtype)


def as_column(row):
    n = row.shape[1]
    return jnp.broadcast_to(row, (n, n)).T


def normalize(raw):
    values = raw.astype(F32)
    scale = lax.rsqrt(jnp.sum(values * values, axis=-1, keepdims=True) + 1e-06)
    return values * scale, scale


def norm_back(unit, scale, upstream):
    return (upstream - unit * jnp.sum(unit * upstream, axis=-1, keepdims=True)) * scale


def matmul_t(a, b):
    return lax.dot_general(a, b, (((1,), (1,)), ((), ())), preferred_element_type=F32)


def matmul(a, b):
    return jnp.dot(a, b, preferred_element_type=F32)


def t_matmul(a, b):
    return lax.dot_general(a, b, (((0,), (0,)), ((), ())), preferred_element_type=F32)


class Scorer:
    def __init__(self, scal_ref, label_ref, place_ref):
        self.temper = jnp.exp(jnp.full((1, 128), scal_ref[0], F32))
        self.bias = scal_ref[1]
        self.labels = label_ref
        self.place = place_ref[0]
        self.columns = {}
        self.sums = None

    def side(self):
        return 1 - 2 * lax.rem(self.place, 2)

    def label_row(self, offset):
        count = self.labels.shape[0]
        at = lax.rem(self.place + offset + count, count)
        return self.labels[pl.ds(at, 1), :]

    def label_column(self, name, offset):
        if name not in self.columns:
            self.columns[name] = as_column(self.label_row(offset).astype(F32))
        return self.columns[name]

    def grads(self, image, text, weight, image_label, text_label, count_it):
        scaled = self.temper * matmul_t(image, text)
        logit = scaled + self.bias
        pos = image_label == text_label.astype(F32)
        small = jnp.exp(-jnp.abs(logit))
        share = 1.0 / (1.0 + small)
        sigmoid = jnp.where(logit >= 0, share, small * share)
        grad = weight * (sigmoid - pos.astype(F32))
        if count_it:
            signed = jnp.where(pos, -logit, logit)
            loss = weight * (jnp.maximum(signed, 0.0) + jnp.log1p(small))
            terms = (loss, grad * scaled, grad)
            self.sums = terms if self.sums is None else tuple(a + b for a, b in zip(self.sums, terms))
        return grad.astype(BF16)


def weight_of(packed, width):
    parts = [packed[:, width + at : width + at + 1].astype(F32) for at in (0, 32, 64)]
    return parts[0] + parts[1] + parts[2]


def prepare(image_ref, text_ref, weight_ref, text_unit_ref, image_pack_ref, both_ref):
    width = image_ref.shape[1]
    v = normalize(text_ref[...])[0].astype(BF16)
    u = normalize(image_ref[...])[0].astype(BF16)
    weight = as_column(weight_ref[...])
    high = weight.astype(BF16)
    rest = weight - high.astype(F32)
    middle = rest.astype(BF16)
    low = (rest - middle.astype(F32)).astype(BF16)
    lane = lax.broadcasted_iota(jnp.int32, weight.shape, 1)
    coded = jnp.where(lane < 32, high.astype(F32), jnp.where(lane < 64, middle.astype(F32), low.astype(F32))).astype(BF16)
    text_unit_ref[...] = v
    image_pack_ref[:, :width] = u
    image_pack_ref[:, width:] = coded
    both_ref[:, :width] = u
    both_ref[:, width : width + 128] = coded
    both_ref[:, width + 128 :] = v


def early_kernel(
    scal_ref, place_ref, label_ref, own_ref, after_ref, before_ref, cross_ref,
    image_total_ref, text_total_ref, far_ref, down_ref, up_ref, sums_ref,
):
    width = cross_ref.shape[1]
    scorer = Scorer(scal_ref, label_ref, place_ref)
    side = scorer.side()
    even = side == 1
    u, v = own_ref[:, :width], own_ref[:, width + 128 :]
    ua, va = after_ref[:, :width], after_ref[:, width + 128 :]
    ub, vb = before_ref[:, :width], before_ref[:, width + 128 :]
    vc = cross_ref[...]
    w, wa, wb = weight_of(own_ref, width), weight_of(after_ref, width), weight_of(before_ref, width)
    row, row_a, row_b = scorer.label_row(0), scorer.label_row(2), scorer.label_row(-2)
    row_c = scorer.label_row(side)
    col, col_a, col_b = as_column(row.astype(F32)), as_column(row_a.astype(F32)), as_column(row_b.astype(F32))
    g0 = scorer.grads(u, v, w, col, row, True)
    ga = scorer.grads(u, va, w, col, row_a, True)
    gb = scorer.grads(u, vb, w, col, row_b, True)
    gc = scorer.grads(u, vc, w, col, row_c, True)
    gfar = scorer.grads(ub, va, wb, col_b, row_a, True)
    ux = jnp.where(even, ub, ua)
    gx = scorer.grads(ux, vc, jnp.where(even, wb, wa), jnp.where(even, col_b, col_a), row_c, True)
    ta = scorer.grads(ua, v, wa, col_a, row, False)
    tb = scorer.grads(ub, v, wb, col_b, row, False)
    image_total_ref[...] = matmul(g0, v) + matmul(ga, va) + matmul(gb, vb) + matmul(gc, vc)
    text_total_ref[...] = t_matmul(g0, u) + t_matmul(ta, ua) + t_matmul(tb, ub)
    far_ref[...] = matmul(gx, vc)
    down_ref[...] = matmul(gfar, va)
    up_ref[...] = t_matmul(gfar, ub)
    sums_ref[...] = jnp.zeros_like(sums_ref)
    for at in range(3):
        sums_ref[at : at + 1, :] = jnp.sum(scorer.sums[at], axis=0, keepdims=True)


def relay_kernel(
    scal_ref, place_ref, label_ref, own_ref, after_ref, before_ref, relay_ref, early_ref,
    near_ref, far_ref, sums_ref,
):
    width = relay_ref.shape[1]
    scorer = Scorer(scal_ref, label_ref, place_ref)
    side = scorer.side()
    even = side == 1
    vr = relay_ref[...]
    row_r = scorer.label_row(-side)
    col = as_column(scorer.label_row(0).astype(F32))
    col_x = as_column(scorer.label_row(2 * side).astype(F32))
    near_ref[...] = scorer.grads(own_ref[:, :width], vr, weight_of(own_ref, width), col, row_r, True)
    ux = jnp.where(even, after_ref[:, :width], before_ref[:, :width])
    wx = jnp.where(even, weight_of(after_ref, width), weight_of(before_ref, width))
    far_ref[...] = scorer.grads(ux, vr, wx, col_x, row_r, True)
    lane = lax.broadcasted_iota(jnp.int32, (1, 128), 1)
    message = jnp.zeros((1, 128), F32)
    for at in range(3):
        total = jnp.sum(scorer.sums[at], axis=0, keepdims=True) + early_ref[at : at + 1, :]
        message = jnp.where(lane == at, jnp.sum(total, axis=1, keepdims=True), message)
    sums_ref[...] = message


def late_kernel(
    scal_ref, place_ref, label_ref, own_ref, after_ref, before_ref, cross_ref, relay_ref, relay_v_ref,
    near_ref, far_g_ref, far_ref, down_in_ref, up_in_ref, image_in_ref, text_in_ref,
    up_ref, down_ref, image_total_ref, text_total_ref,
):
    width = relay_v_ref.shape[1]
    rows = relay_v_ref.shape[0]
    scorer = Scorer(scal_ref, label_ref, place_ref)
    side = scorer.side()
    even = side == 1
    v = own_ref[:, width + 128 :]
    va, vb = after_ref[:, width + 128 :], before_ref[:, width + 128 :]
    uc, ur = cross_ref[:, :width], relay_ref[:, :width]
    wc, wr = weight_of(cross_ref, width), weight_of(relay_ref, width)
    col_c = as_column(scorer.label_row(side).astype(F32))
    col_r = as_column(scorer.label_row(-side).astype(F32))
    row, row_a, row_b = scorer.label_row(0), scorer.label_row(2), scorer.label_row(-2)
    gcx = scorer.grads(uc, jnp.where(even, vb, va), wc, col_c, jnp.where(even, row_b, row_a), False)
    grx = scorer.grads(ur, jnp.where(even, va, vb), wr, col_r, jnp.where(even, row_a, row_b), False)
    far_text_c = t_matmul(gcx, uc)
    far_text_r = t_matmul(grx, ur)
    far_image_c = far_ref[...]
    far_image_r = matmul(far_g_ref[...], relay_v_ref[...])
    up_ref[:rows, :] = jnp.where(even, far_image_r, far_image_c).astype(BF16)
    up_ref[rows:, :] = (up_in_ref[...] + jnp.where(even, far_text_r, far_text_c)).astype(BF16)
    down_ref[:rows, :] = (down_in_ref[...] + jnp.where(even, far_image_c, far_image_r)).astype(BF16)
    down_ref[rows:, :] = jnp.where(even, far_text_c, far_text_r).astype(BF16)
    gc = scorer.grads(uc, v, wc, col_c, row, False)
    gr = scorer.grads(ur, v, wr, col_r, row, False)
    image_total_ref[...] = image_in_ref[...] + matmul(near_ref[...], relay_v_ref[...])
    text_total_ref[...] = text_in_ref[...] + t_matmul(gc, uc) + t_matmul(gr, ur)


def final_kernel(scal_ref, image_ref, text_ref, image_total_ref, text_total_ref, up_ref, down_ref, image_grad_ref, text_grad_ref):
    rows, width = image_ref.shape
    temper = jnp.exp(jnp.full((1, 128), scal_ref[0], F32))[:, :1]
    for raw_ref, total_ref, out_ref, at in (
        (image_ref, image_total_ref, image_grad_ref, 0),
        (text_ref, text_total_ref, text_grad_ref, rows),
    ):
        total = total_ref[...] + up_ref[at : at + rows, :].astype(F32) + down_ref[at : at + rows, :].astype(F32)
        unit, scale = normalize(raw_ref[...])
        out_ref[...] = norm_back(unit, scale, temper * total).astype(BF16)


def call(kernel, ins, outs, name):
    return pl.pallas_call(
        kernel,
        out_shape=outs,
        in_specs=ins,
        out_specs=jax.tree.map(lambda _: VMEM, outs),
        compiler_params=PARAMS,
        name=name,
    )


def summed_over(axis, row):
    count = lax.axis_size(axis)
    sent = jnp.broadcast_to(row.reshape(1, 1, 128), (count, 1, 128))
    return jnp.sum(lax.all_to_all(sent, axis, 0, 0), axis=0)


def per_device(images, texts, labels, weights, log_temp, bias):
    cycle = lax.axis_size("blk")
    groups = lax.axis_size("group")
    rows, width = images.shape
    place = lax.axis_index("blk").astype(jnp.int32).reshape(1)
    scal = jnp.concatenate([log_temp, bias])
    head = [SMEM, SMEM, VMEM]

    def passed(value, step_of):
        return lax.ppermute(value, "blk", [(p, (p + step_of(p)) % cycle) for p in range(cycle)])

    def across(value):
        return passed(value, lambda p: 1 - 2 * (p % 2))

    def relayed(value):
        return passed(value, lambda p: 2 - 4 * (p % 2))

    def upward(value):
        return passed(value, lambda p: 2)

    def downward(value):
        return passed(value, lambda p: -2)

    block = shape(rows, width, F32)
    text_unit, image_pack, both = call(
        prepare,
        [VMEM] * 3,
        (shape(rows, width, BF16), shape(rows, width + 128, BF16), shape(rows, 2 * width + 128, BF16)),
        "prepare",
    )(images, texts, weights.reshape(1, rows))
    cross_v = across(text_unit)
    after = downward(both)
    before = upward(both)
    cross_u = across(image_pack)
    relay_v = relayed(cross_v)
    image_total, text_total, far, far_down, far_up, early = call(
        early_kernel, head + [VMEM] * 4, (block,) * 5 + (shape(8, 128, F32),), "early"
    )(scal, place, labels, both, after, before, cross_v)
    relay_u = relayed(cross_u)
    near_g, far_g, sums = call(
        relay_kernel, head + [VMEM] * 5, (shape(rows, rows, BF16),) * 2 + (shape(1, 128, F32),), "relay"
    )(scal, place, labels, both, after, before, relay_v, early)
    sums = summed_over("group", sums)
    to_up, to_down, image_total, text_total = call(
        late_kernel, head + [VMEM] * 13, (shape(2 * rows, width, BF16),) * 2 + (block,) * 2, "late"
    )(scal, place, labels, both, after, before, cross_u, relay_u, relay_v, near_g, far_g, far, far_down, far_up, image_total, text_total)
    from_below = upward(to_up)
    from_above = downward(to_down)
    sums = summed_over("blk", sums)
    image_grad, text_grad = call(
        final_kernel, [SMEM] + [VMEM] * 6, (shape(rows, width, BF16),) * 2, "final"
    )(scal, images, texts, image_total, text_total, from_below, from_above)
    count = float(cycle * groups * rows) * float(rows) * 8.0
    return image_grad, text_grad, sums.reshape(128)[:3] / count


def solution(mesh):
    rows = P(("blk", "group"), None)
    in_specs = (rows, rows, P(None, "group"), P(("blk", "group")), P(), P())
    return jax.shard_map(per_device, mesh=mesh, in_specs=in_specs, out_specs=(rows, rows, P()), check_vma=False)
```

```python
import functools

import jax
import jax.numpy as jnp
from jax import lax
from jax.experimental import pallas as pl
from jax.experimental.pallas import tpu as pltpu
from jax.sharding import PartitionSpec as P

VMEM = pl.BlockSpec(memory_space=pltpu.VMEM)
SMEM = pl.BlockSpec(memory_space=pltpu.SMEM)
F32 = jnp.float32
BF16 = jnp.bfloat16
PARAMS = pltpu.CompilerParams(vmem_limit_bytes=16 * 1024 * 1024)


def shape(rows, cols, dtype):
    return jax.ShapeDtypeStruct((rows, cols), dtype)


def as_column(row):
    n = row.shape[1]
    return jnp.broadcast_to(row, (n, n)).T


def normalize(raw):
    values = raw.astype(F32)
    scale = lax.rsqrt(jnp.sum(values * values, axis=-1, keepdims=True) + 1e-06)
    return values * scale, scale


def norm_back(unit, scale, upstream):
    return (upstream - unit * jnp.sum(unit * upstream, axis=-1, keepdims=True)) * scale


def matmul_t(a, b):
    return lax.dot_general(a, b, (((1,), (1,)), ((), ())), preferred_element_type=F32)


def matmul(a, b):
    return jnp.dot(a, b, preferred_element_type=F32)


def t_matmul(a, b):
    return lax.dot_general(a, b, (((0,), (0,)), ((), ())), preferred_element_type=F32)


class Scorer:
    def __init__(self, scal_ref, label_ref, place_ref):
        self.temper = jnp.exp(jnp.full((1, 128), scal_ref[0], F32))
        self.bias = scal_ref[1]
        self.labels = label_ref
        self.place = place_ref[0]
        self.columns = {}
        self.sums = None

    def side(self):
        return 1 - 2 * lax.rem(self.place, 2)

    def label_row(self, offset):
        count = self.labels.shape[0]
        at = lax.rem(self.place + offset + count, count)
        return self.labels[pl.ds(at, 1), :]

    def label_column(self, name, offset):
        if name not in self.columns:
            self.columns[name] = as_column(self.label_row(offset).astype(F32))
        return self.columns[name]

    def grads(self, image, text, weight, image_label, text_label, count_it):
        scaled = self.temper * matmul_t(image, text)
        logit = scaled + self.bias
        pos = image_label == text_label.astype(F32)
        small = jnp.exp(-jnp.abs(logit))
        share = 1.0 / (1.0 + small)
        sigmoid = jnp.where(logit >= 0, share, small * share)
        grad = weight * (sigmoid - pos.astype(F32))
        if count_it:
            signed = jnp.where(pos, -logit, logit)
            loss = weight * (jnp.maximum(signed, 0.0) + jnp.log1p(small))
            terms = (loss, grad * scaled, grad)
            self.sums = terms if self.sums is None else tuple(a + b for a, b in zip(self.sums, terms))
        return grad.astype(BF16)

    def store_sums(self, out_ref, more_ref=None):
        out_ref[...] = jnp.zeros_like(out_ref) if more_ref is None else more_ref[...]
        for at in range(3):
            out_ref[at : at + 1, :] += jnp.sum(self.sums[at], axis=0, keepdims=True)


def weight_of(packed, width):
    parts = [packed[:, width + at : width + at + 1].astype(F32) for at in (0, 32, 64)]
    return parts[0] + parts[1] + parts[2]


def text_kernel(text_ref, text_unit_ref):
    text_unit_ref[...] = normalize(text_ref[...])[0].astype(BF16)


def image_kernel(image_ref, weight_ref, text_unit_ref, image_pack_ref, both_ref):
    width = image_ref.shape[1]
    u = normalize(image_ref[...])[0].astype(BF16)
    weight = as_column(weight_ref[...])
    high = weight.astype(BF16)
    rest = weight - high.astype(F32)
    middle = rest.astype(BF16)
    low = (rest - middle.astype(F32)).astype(BF16)
    lane = lax.broadcasted_iota(jnp.int32, weight.shape, 1)
    coded = jnp.where(lane < 32, high.astype(F32), jnp.where(lane < 64, middle.astype(F32), low.astype(F32))).astype(BF16)
    image_pack_ref[:, :width] = u
    image_pack_ref[:, width:] = coded
    both_ref[:, :width] = u
    both_ref[:, width : width + 128] = coded
    both_ref[:, width + 128 :] = text_unit_ref[...]


def own_kernel(scal_ref, place_ref, label_ref, own_ref, cross_ref, image_total_ref, text_total_ref, sums_ref):
    width = cross_ref.shape[1]
    scorer = Scorer(scal_ref, label_ref, place_ref)
    u, v = own_ref[:, :width], own_ref[:, width + 128 :]
    vc = cross_ref[...]
    w = weight_of(own_ref, width)
    row = scorer.label_row(0)
    col = as_column(row.astype(F32))
    g0 = scorer.grads(u, v, w, col, row, True)
    gc = scorer.grads(u, vc, w, col, scorer.label_row(scorer.side()), True)
    image_total_ref[...] = matmul(g0, v) + matmul(gc, vc)
    text_total_ref[...] = t_matmul(g0, u)
    scorer.store_sums(sums_ref)


def early_kernel(
    scal_ref, place_ref, label_ref, own_ref, after_ref, before_ref, cross_ref,
    image_in_ref, text_in_ref, sums_in_ref,
    image_total_ref, text_total_ref, far_ref, down_ref, up_ref, sums_ref,
):
    width = cross_ref.shape[1]
    scorer = Scorer(scal_ref, label_ref, place_ref)
    side = scorer.side()
    even = side == 1
    u, v = own_ref[:, :width], own_ref[:, width + 128 :]
    ua, va = after_ref[:, :width], after_ref[:, width + 128 :]
    ub, vb = before_ref[:, :width], before_ref[:, width + 128 :]
    vc = cross_ref[...]
    w, wa, wb = weight_of(own_ref, width), weight_of(after_ref, width), weight_of(before_ref, width)
    row, row_a, row_b = scorer.label_row(0), scorer.label_row(2), scorer.label_row(-2)
    row_c = scorer.label_row(side)
    col, col_a, col_b = as_column(row.astype(F32)), as_column(row_a.astype(F32)), as_column(row_b.astype(F32))
    ga = scorer.grads(u, va, w, col, row_a, True)
    gb = scorer.grads(u, vb, w, col, row_b, True)
    gfar = scorer.grads(ub, va, wb, col_b, row_a, True)
    ux = jnp.where(even, ub, ua)
    gx = scorer.grads(ux, vc, jnp.where(even, wb, wa), jnp.where(even, col_b, col_a), row_c, True)
    ta = scorer.grads(ua, v, wa, col_a, row, False)
    tb = scorer.grads(ub, v, wb, col_b, row, False)
    image_total_ref[...] = image_in_ref[...] + matmul(ga, va) + matmul(gb, vb)
    text_total_ref[...] = text_in_ref[...] + t_matmul(ta, ua) + t_matmul(tb, ub)
    far_ref[...] = matmul(gx, vc)
    down_ref[...] = matmul(gfar, va)
    up_ref[...] = t_matmul(gfar, ub)
    scorer.store_sums(sums_ref, sums_in_ref)


def relay_kernel(
    scal_ref, place_ref, label_ref, own_ref, after_ref, before_ref, relay_ref, early_ref,
    near_ref, far_ref, sums_ref,
):
    width = relay_ref.shape[1]
    scorer = Scorer(scal_ref, label_ref, place_ref)
    side = scorer.side()
    even = side == 1
    vr = relay_ref[...]
    row_r = scorer.label_row(-side)
    col = as_column(scorer.label_row(0).astype(F32))
    col_x = as_column(scorer.label_row(2 * side).astype(F32))
    near_ref[...] = scorer.grads(own_ref[:, :width], vr, weight_of(own_ref, width), col, row_r, True)
    ux = jnp.where(even, after_ref[:, :width], before_ref[:, :width])
    wx = jnp.where(even, weight_of(after_ref, width), weight_of(before_ref, width))
    far_ref[...] = scorer.grads(ux, vr, wx, col_x, row_r, True)
    lane = lax.broadcasted_iota(jnp.int32, (1, 128), 1)
    message = jnp.zeros((1, 128), F32)
    for at in range(3):
        total = jnp.sum(scorer.sums[at], axis=0, keepdims=True) + early_ref[at : at + 1, :]
        message = jnp.where(lane == at, jnp.sum(total, axis=1, keepdims=True), message)
    sums_ref[...] = message


def late_kernel(
    scal_ref, place_ref, label_ref, own_ref, after_ref, before_ref, cross_ref, relay_ref, relay_v_ref,
    near_ref, far_g_ref, far_ref, down_in_ref, up_in_ref, image_in_ref, text_in_ref, got_ref,
    up_ref, down_ref, image_total_ref, text_total_ref, sums_ref,
):
    width = relay_v_ref.shape[1]
    rows = relay_v_ref.shape[0]
    scorer = Scorer(scal_ref, label_ref, place_ref)
    side = scorer.side()
    even = side == 1
    v = own_ref[:, width + 128 :]
    va, vb = after_ref[:, width + 128 :], before_ref[:, width + 128 :]
    uc, ur = cross_ref[:, :width], relay_ref[:, :width]
    wc, wr = weight_of(cross_ref, width), weight_of(relay_ref, width)
    col_c = as_column(scorer.label_row(side).astype(F32))
    col_r = as_column(scorer.label_row(-side).astype(F32))
    row, row_a, row_b = scorer.label_row(0), scorer.label_row(2), scorer.label_row(-2)
    gcx = scorer.grads(uc, jnp.where(even, vb, va), wc, col_c, jnp.where(even, row_b, row_a), False)
    grx = scorer.grads(ur, jnp.where(even, va, vb), wr, col_r, jnp.where(even, row_a, row_b), False)
    far_text_c = t_matmul(gcx, uc)
    far_text_r = t_matmul(grx, ur)
    far_image_c = far_ref[...]
    far_image_r = matmul(far_g_ref[...], relay_v_ref[...])
    up_ref[:rows, :] = jnp.where(even, far_image_r, far_image_c).astype(BF16)
    up_ref[rows:, :] = (up_in_ref[...] + jnp.where(even, far_text_r, far_text_c)).astype(BF16)
    down_ref[:rows, :] = (down_in_ref[...] + jnp.where(even, far_image_c, far_image_r)).astype(BF16)
    down_ref[rows:, :] = jnp.where(even, far_text_c, far_text_r).astype(BF16)
    gc = scorer.grads(uc, v, wc, col_c, row, False)
    gr = scorer.grads(ur, v, wr, col_r, row, False)
    image_total_ref[...] = image_in_ref[...] + matmul(near_ref[...], relay_v_ref[...])
    text_total_ref[...] = text_in_ref[...] + t_matmul(gc, uc) + t_matmul(gr, ur)
    sums_ref[...] = jnp.sum(got_ref[...], axis=0, keepdims=True)


def final_kernel(
    count, scal_ref, image_ref, text_ref, image_total_ref, text_total_ref, up_ref, down_ref, got_ref,
    image_grad_ref, text_grad_ref, stats_ref,
):
    rows, width = image_ref.shape
    temper = jnp.exp(jnp.full((1, 128), scal_ref[0], F32))[:, :1]
    for raw_ref, total_ref, out_ref, at in (
        (image_ref, image_total_ref, image_grad_ref, 0),
        (text_ref, text_total_ref, text_grad_ref, rows),
    ):
        total = total_ref[...] + up_ref[at : at + rows, :].astype(F32) + down_ref[at : at + rows, :].astype(F32)
        unit, scale = normalize(raw_ref[...])
        out_ref[...] = norm_back(unit, scale, temper * total).astype(BF16)
    got = jnp.sum(got_ref[...], axis=0, keepdims=True) / count
    for at in range(3):
        stats_ref[at] = got[0, at]


def call(kernel, ins, outs, name, work, out_specs=None):
    return pl.pallas_call(
        kernel,
        out_shape=outs,
        in_specs=ins,
        out_specs=jax.tree.map(lambda _: VMEM, outs) if out_specs is None else out_specs,
        compiler_params=PARAMS,
        cost_estimate=pl.CostEstimate(flops=work, bytes_accessed=0, transcendentals=0),
        name=name,
    )


def exchanged(row, axis):
    count = lax.axis_size(axis)
    sent = jnp.broadcast_to(row.reshape(1, 1, 128), (count, 1, 128))
    return lax.all_to_all(sent, axis, 0, 0).reshape(count, 128)


def per_device(images, texts, labels, weights, log_temp, bias):
    cycle = lax.axis_size("blk")
    groups = lax.axis_size("group")
    rows, width = images.shape
    place = lax.axis_index("blk").astype(jnp.int32).reshape(1)
    scal = jnp.concatenate([log_temp, bias])
    head = [SMEM, SMEM, VMEM]
    dot = 2 * rows * rows * width

    def passed(value, step_of):
        return lax.ppermute(value, "blk", [(p, (p + step_of(p)) % cycle) for p in range(cycle)])

    def across(value):
        return passed(value, lambda p: 1 - 2 * (p % 2))

    def relayed(value):
        return passed(value, lambda p: 2 - 4 * (p % 2))

    def upward(value):
        return passed(value, lambda p: 2)

    def downward(value):
        return passed(value, lambda p: -2)

    block = shape(rows, width, F32)
    text_unit = call(text_kernel, [VMEM], shape(rows, width, BF16), "text", 10 * dot)(texts)
    cross_v = across(text_unit)
    image_pack, both = call(
        image_kernel,
        [VMEM] * 3,
        (shape(rows, width + 128, BF16), shape(rows, 2 * width + 128, BF16)),
        "image",
        10 * dot,
    )(images, weights.reshape(1, rows), text_unit)
    after = downward(both)
    before = upward(both)
    cross_u = across(image_pack)
    relay_v = relayed(cross_v)
    image_total, text_total, sums = call(
        own_kernel, head + [VMEM] * 2, (block,) * 2 + (shape(8, 128, F32),), "own", 150 * dot
    )(scal, place, labels, both, cross_v)
    image_total, text_total, far, far_down, far_up, sums = call(
        early_kernel, head + [VMEM] * 7, (block,) * 5 + (shape(8, 128, F32),), "early", 20 * dot
    )(scal, place, labels, both, after, before, cross_v, image_total, text_total, sums)
    cross_u, sums = lax.optimization_barrier((cross_u, sums))
    relay_u = relayed(cross_u)
    near_g, far_g, sums = call(
        relay_kernel, head + [VMEM] * 5, (shape(rows, rows, BF16),) * 2 + (shape(1, 128, F32),), "relay", 10 * dot
    )(scal, place, labels, both, after, before, relay_v, sums)
    got = exchanged(sums, "group")
    to_up, to_down, image_total, text_total, sums = call(
        late_kernel,
        head + [VMEM] * 14,
        (shape(2 * rows, width, BF16),) * 2 + (block,) * 2 + (shape(1, 128, F32),),
        "late",
        20 * dot,
    )(
        scal, place, labels, both, after, before, cross_u, relay_u, relay_v,
        near_g, far_g, far, far_down, far_up, image_total, text_total, got,
    )
    from_below = upward(to_up)
    from_above = downward(to_down)
    got = exchanged(sums, "blk")
    count = float(cycle * groups * rows) * float(rows) * 8.0
    image_grad, text_grad, stats = call(
        functools.partial(final_kernel, count),
        [SMEM] + [VMEM] * 7,
        (shape(rows, width, BF16),) * 2 + (jax.ShapeDtypeStruct((3,), F32),),
        "final",
        10 * dot,
        (VMEM, VMEM, SMEM),
    )(scal, images, texts, image_total, text_total, from_below, from_above, got)
    return image_grad, text_grad, stats


def solution(mesh):
    rows = P(("blk", "group"), None)
    in_specs = (rows, rows, P(None, "group"), P(("blk", "group")), P(), P())
    return jax.shard_map(per_device, mesh=mesh, in_specs=in_specs, out_specs=(rows, rows, P()), check_vma=False)
```

```python
import functools

import jax
import jax.numpy as jnp
from jax import lax
from jax.experimental import pallas as pl
from jax.experimental.pallas import tpu as pltpu
from jax.sharding import PartitionSpec as P

VMEM = pl.BlockSpec(memory_space=pltpu.VMEM)
SMEM = pl.BlockSpec(memory_space=pltpu.SMEM)
F32 = jnp.float32
BF16 = jnp.bfloat16
PARAMS = pltpu.CompilerParams(vmem_limit_bytes=16 * 1024 * 1024)


def shape(rows, cols, dtype):
    return jax.ShapeDtypeStruct((rows, cols), dtype)


def as_column(row):
    n = row.shape[1]
    return jnp.broadcast_to(row, (n, n)).T


def normalize(raw):
    values = raw.astype(F32)
    scale = lax.rsqrt(jnp.sum(values * values, axis=-1, keepdims=True) + 1e-06)
    return values * scale, scale


def norm_back(unit, scale, upstream):
    return (upstream - unit * jnp.sum(unit * upstream, axis=-1, keepdims=True)) * scale


def matmul_t(a, b):
    return lax.dot_general(a, b, (((1,), (1,)), ((), ())), preferred_element_type=F32)


def matmul(a, b):
    return jnp.dot(a, b, preferred_element_type=F32)


def t_matmul(a, b):
    return lax.dot_general(a, b, (((0,), (0,)), ((), ())), preferred_element_type=F32)


class Scorer:
    def __init__(self, scal_ref, label_ref, place_ref):
        self.temper = jnp.exp(jnp.full((1, 128), scal_ref[0], F32))
        self.bias = scal_ref[1]
        self.labels = label_ref
        self.place = place_ref[0]
        self.columns = {}
        self.sums = None

    def side(self):
        return 1 - 2 * lax.rem(self.place, 2)

    def label_row(self, offset):
        count = self.labels.shape[0]
        at = lax.rem(self.place + offset + count, count)
        return self.labels[pl.ds(at, 1), :]

    def label_column(self, name, offset):
        if name not in self.columns:
            self.columns[name] = as_column(self.label_row(offset).astype(F32))
        return self.columns[name]

    def grads(self, image, text, weight, image_label, text_label, count_it):
        scaled = self.temper * matmul_t(image, text)
        logit = scaled + self.bias
        pos = image_label == text_label.astype(F32)
        small = jnp.exp(-jnp.abs(logit))
        share = 1.0 / (1.0 + small)
        sigmoid = jnp.where(logit >= 0, share, small * share)
        grad = weight * (sigmoid - pos.astype(F32))
        if count_it:
            signed = jnp.where(pos, -logit, logit)
            loss = weight * (jnp.maximum(signed, 0.0) + jnp.log1p(small))
            terms = (loss, grad * scaled, grad)
            self.sums = terms if self.sums is None else tuple(a + b for a, b in zip(self.sums, terms))
        return grad.astype(BF16)

    def store_sums(self, out_ref, more_ref=None):
        out_ref[...] = jnp.zeros_like(out_ref) if more_ref is None else more_ref[...]
        for at in range(3):
            out_ref[at : at + 1, :] += jnp.sum(self.sums[at], axis=0, keepdims=True)


def weight_of(packed, width):
    parts = [packed[:, width + at : width + at + 1].astype(F32) for at in (0, 32, 64)]
    return parts[0] + parts[1] + parts[2]


def text_kernel(text_ref, text_unit_ref):
    text_unit_ref[...] = normalize(text_ref[...])[0].astype(BF16)


def image_kernel(image_ref, weight_ref, text_unit_ref, both_ref):
    width = image_ref.shape[1]
    weight = as_column(weight_ref[...])
    high = weight.astype(BF16)
    rest = weight - high.astype(F32)
    middle = rest.astype(BF16)
    low = (rest - middle.astype(F32)).astype(BF16)
    lane = lax.broadcasted_iota(jnp.int32, weight.shape, 1)
    coded = jnp.where(lane < 32, high.astype(F32), jnp.where(lane < 64, middle.astype(F32), low.astype(F32)))
    both_ref[:, :width] = normalize(image_ref[...])[0].astype(BF16)
    both_ref[:, width : width + 128] = coded.astype(BF16)
    both_ref[:, width + 128 :] = text_unit_ref[...]


def own_kernel(
    scal_ref, place_ref, label_ref, own_ref, cross_ref,
    image_total_ref, text_total_ref, cross_total_ref, sums_ref,
):
    width = cross_ref.shape[1]
    scorer = Scorer(scal_ref, label_ref, place_ref)
    u, v = own_ref[:, :width], own_ref[:, width + 128 :]
    vc = cross_ref[...]
    w = weight_of(own_ref, width)
    row = scorer.label_row(0)
    col = as_column(row.astype(F32))
    g0 = scorer.grads(u, v, w, col, row, True)
    gc = scorer.grads(u, vc, w, col, scorer.label_row(scorer.side()), True)
    image_total_ref[...] = matmul(g0, v) + matmul(gc, vc)
    text_total_ref[...] = t_matmul(g0, u)
    cross_total_ref[...] = t_matmul(gc, u)
    scorer.store_sums(sums_ref)


def early_kernel(
    scal_ref, place_ref, label_ref, own_ref, after_ref, before_ref, cross_ref,
    image_in_ref, text_in_ref, cross_in_ref, sums_in_ref,
    image_total_ref, text_total_ref, cross_total_ref, far_ref, down_ref, up_ref, sums_ref,
):
    width = cross_ref.shape[1]
    scorer = Scorer(scal_ref, label_ref, place_ref)
    side = scorer.side()
    even = side == 1
    u, v = own_ref[:, :width], own_ref[:, width + 128 :]
    ua, va = after_ref[:, :width], after_ref[:, width + 128 :]
    ub, vb = before_ref[:, :width], before_ref[:, width + 128 :]
    vc = cross_ref[...]
    w, wa, wb = weight_of(own_ref, width), weight_of(after_ref, width), weight_of(before_ref, width)
    row, row_a, row_b = scorer.label_row(0), scorer.label_row(2), scorer.label_row(-2)
    row_c = scorer.label_row(side)
    col, col_a, col_b = as_column(row.astype(F32)), as_column(row_a.astype(F32)), as_column(row_b.astype(F32))
    ux, wx, col_x = jnp.where(even, ub, ua), jnp.where(even, wb, wa), jnp.where(even, col_b, col_a)
    un, wn, col_n = jnp.where(even, ua, ub), jnp.where(even, wa, wb), jnp.where(even, col_a, col_b)
    gx = scorer.grads(ux, vc, wx, col_x, row_c, True)
    gn = scorer.grads(un, vc, wn, col_n, row_c, False)
    cross_total_ref[...] = (cross_in_ref[...] + t_matmul(gx, ux) + t_matmul(gn, un)).astype(BF16)
    far_ref[...] = matmul(gx, vc)
    ga = scorer.grads(u, va, w, col, row_a, True)
    gb = scorer.grads(u, vb, w, col, row_b, True)
    gfar = scorer.grads(ub, va, wb, col_b, row_a, True)
    ta = scorer.grads(ua, v, wa, col_a, row, False)
    tb = scorer.grads(ub, v, wb, col_b, row, False)
    image_total_ref[...] = image_in_ref[...] + matmul(ga, va) + matmul(gb, vb)
    text_total_ref[...] = text_in_ref[...] + t_matmul(ta, ua) + t_matmul(tb, ub)
    down_ref[...] = matmul(gfar, va)
    up_ref[...] = t_matmul(gfar, ub).astype(BF16)
    scorer.store_sums(sums_ref, sums_in_ref)


def diagonal_kernel(
    scal_ref, place_ref, label_ref, own_ref, after_ref, before_ref, diagonal_ref, early_ref,
    near_ref, far_ref, sums_ref,
):
    width = diagonal_ref.shape[1]
    scorer = Scorer(scal_ref, label_ref, place_ref)
    side = scorer.side()
    even = side == 1
    vr = diagonal_ref[...]
    row_r = scorer.label_row(-side)
    col = as_column(scorer.label_row(0).astype(F32))
    col_x = as_column(scorer.label_row(2 * side).astype(F32))
    near_ref[...] = scorer.grads(own_ref[:, :width], vr, weight_of(own_ref, width), col, row_r, True)
    ux = jnp.where(even, after_ref[:, :width], before_ref[:, :width])
    wx = jnp.where(even, weight_of(after_ref, width), weight_of(before_ref, width))
    far_ref[...] = scorer.grads(ux, vr, wx, col_x, row_r, True)
    lane = lax.broadcasted_iota(jnp.int32, (1, 128), 1)
    message = jnp.zeros((1, 128), F32)
    for at in range(3):
        total = jnp.sum(scorer.sums[at], axis=0, keepdims=True) + early_ref[at : at + 1, :]
        message = jnp.where(lane == at, jnp.sum(total, axis=1, keepdims=True), message)
    sums_ref[...] = message


def late_kernel(
    place_ref, after_ref, before_ref, diagonal_ref, near_g_ref, far_g_ref, far_ref, down_in_ref, up_in_ref, image_in_ref,
    text_in_ref, cross_ref, got_ref,
    up_ref, down_ref, back_ref, image_total_ref, text_total_ref, sums_ref,
):
    rows, width = diagonal_ref.shape
    even = lax.rem(place_ref[0], 2) == 0
    vr = diagonal_ref[...]
    g = far_g_ref[...]
    back_ref[...] = t_matmul(g, jnp.where(even, after_ref[:, :width], before_ref[:, :width])).astype(BF16)
    far_cross = far_ref[...]
    far_diagonal = matmul(g, vr)
    up_ref[:rows, :] = jnp.where(even, far_diagonal, far_cross).astype(BF16)
    up_ref[rows:, :] = up_in_ref[...]
    down_ref[...] = (down_in_ref[...] + jnp.where(even, far_cross, far_diagonal)).astype(BF16)
    image_total_ref[...] = image_in_ref[...] + matmul(near_g_ref[...], vr)
    text_total_ref[...] = text_in_ref[...] + cross_ref[...].astype(F32)
    sums_ref[...] = jnp.sum(got_ref[...], axis=0, keepdims=True)


def final_kernel(
    count, scal_ref, image_ref, text_ref, image_total_ref, text_total_ref,
    up_ref, down_ref, back_ref, got_ref,
    image_grad_ref, text_grad_ref, stats_ref,
):
    rows, width = image_ref.shape
    temper = jnp.exp(jnp.full((1, 128), scal_ref[0], F32))[:, :1]
    image_total = image_total_ref[...] + up_ref[:rows, :].astype(F32) + down_ref[...].astype(F32)
    text_total = text_total_ref[...] + up_ref[rows:, :].astype(F32) + back_ref[...].astype(F32)
    for raw_ref, total, out_ref in ((image_ref, image_total, image_grad_ref), (text_ref, text_total, text_grad_ref)):
        unit, scale = normalize(raw_ref[...])
        out_ref[...] = norm_back(unit, scale, temper * total).astype(BF16)
    got = jnp.sum(got_ref[...], axis=0, keepdims=True) / count
    for at in range(3):
        stats_ref[at] = got[0, at]


def call(kernel, ins, outs, name, work, out_specs=None):
    return pl.pallas_call(
        kernel,
        out_shape=outs,
        in_specs=ins,
        out_specs=jax.tree.map(lambda _: VMEM, outs) if out_specs is None else out_specs,
        compiler_params=PARAMS,
        cost_estimate=pl.CostEstimate(flops=work, bytes_accessed=0, transcendentals=0),
        name=name,
    )


def exchanged(row, axis):
    count = lax.axis_size(axis)
    sent = jnp.broadcast_to(row.reshape(1, 1, 128), (count, 1, 128))
    return lax.all_to_all(sent, axis, 0, 0).reshape(count, 128)


def per_device(images, texts, labels, weights, log_temp, bias):
    cycle = lax.axis_size("blk")
    groups = lax.axis_size("group")
    rows, width = images.shape
    place = lax.axis_index("blk").astype(jnp.int32).reshape(1)
    scal = jnp.concatenate([log_temp, bias])
    head = [SMEM, SMEM, VMEM]
    dot = 2 * rows * rows * width

    def passed(value, step_of):
        return lax.ppermute(value, "blk", [(p, (p + step_of(p)) % cycle) for p in range(cycle)])

    def across(value):
        return passed(value, lambda p: 1 - 2 * (p % 2))

    def diagonally(value):
        return passed(value, lambda p: 2 * (p % 2) - 1)

    def upward(value):
        return passed(value, lambda p: 2)

    def downward(value):
        return passed(value, lambda p: -2)

    block, half = shape(rows, width, F32), shape(rows, width, BF16)
    text_unit = call(text_kernel, [VMEM], half, "text", 10 * dot)(texts)
    cross_v = across(text_unit)
    diagonal_v = diagonally(text_unit)
    both = call(image_kernel, [VMEM] * 3, shape(rows, 2 * width + 128, BF16), "image", 10 * dot)(
        images, weights.reshape(1, rows), text_unit
    )
    after = downward(both)
    before = upward(both)
    image_total, text_total, cross_total, sums = call(
        own_kernel, head + [VMEM] * 2, (block,) * 3 + (shape(8, 128, F32),), "own", 200 * dot
    )(scal, place, labels, both, cross_v)
    image_total, text_total, cross_total, far, far_down, far_up, sums = call(
        early_kernel,
        head + [VMEM] * 8,
        (block, block, half, block, block, half, shape(8, 128, F32)),
        "early",
        20 * dot,
    )(scal, place, labels, both, after, before, cross_v, image_total, text_total, cross_total, sums)
    from_cross = across(cross_total)
    near_g, far_g, sums = call(
        diagonal_kernel, head + [VMEM] * 5, (shape(rows, rows, BF16),) * 2 + (shape(1, 128, F32),), "diagonal", 10 * dot
    )(scal, place, labels, both, after, before, diagonal_v, sums)
    got = exchanged(sums, "group")
    to_up, to_down, to_back, image_total, text_total, sums = call(
        late_kernel,
        [SMEM] + [VMEM] * 12,
        (shape(2 * rows, width, BF16), half, half, block, block, shape(1, 128, F32)),
        "late",
        20 * dot,
    )(
        place, after, before, diagonal_v, near_g, far_g, far, far_down, far_up, image_total,
        text_total, from_cross, got,
    )
    from_diagonal = diagonally(to_back)
    from_below = upward(to_up)
    from_above = downward(to_down)
    got = exchanged(sums, "blk")
    count = float(cycle * groups * rows) * float(rows) * 8.0
    image_grad, text_grad, stats = call(
        functools.partial(final_kernel, count),
        [SMEM] + [VMEM] * 8,
        (half, half, jax.ShapeDtypeStruct((3,), F32)),
        "final",
        10 * dot,
        (VMEM, VMEM, SMEM),
    )(scal, images, texts, image_total, text_total, from_below, from_above, from_diagonal, got)
    return image_grad, text_grad, stats


def solution(mesh):
    rows = P(("blk", "group"), None)
    in_specs = (rows, rows, P(None, "group"), P(("blk", "group")), P(), P())
    return jax.shard_map(per_device, mesh=mesh, in_specs=in_specs, out_specs=(rows, rows, P()), check_vma=False)
```

```python
import functools

import jax
import jax.numpy as jnp
from jax import lax
from jax.experimental import pallas as pl
from jax.experimental.pallas import tpu as pltpu
from jax.sharding import PartitionSpec as P

VMEM = pl.BlockSpec(memory_space=pltpu.VMEM)
SMEM = pl.BlockSpec(memory_space=pltpu.SMEM)
F32 = jnp.float32
BF16 = jnp.bfloat16
PARAMS = pltpu.CompilerParams(vmem_limit_bytes=16 * 1024 * 1024)


def shape(rows, cols, dtype):
    return jax.ShapeDtypeStruct((rows, cols), dtype)


def as_column(row):
    n = row.shape[1]
    return jnp.broadcast_to(row, (n, n)).T


def normalize(raw):
    values = raw.astype(F32)
    scale = lax.rsqrt(jnp.sum(values * values, axis=-1, keepdims=True) + 1e-06)
    return values * scale, scale


def norm_back(unit, scale, upstream):
    return (upstream - unit * jnp.sum(unit * upstream, axis=-1, keepdims=True)) * scale


def matmul_t(a, b):
    return lax.dot_general(a, b, (((1,), (1,)), ((), ())), preferred_element_type=F32)


def matmul(a, b):
    return jnp.dot(a, b, preferred_element_type=F32)


def t_matmul(a, b):
    return lax.dot_general(a, b, (((0,), (0,)), ((), ())), preferred_element_type=F32)


class Scorer:
    def __init__(self, scal_ref, label_ref, place_ref):
        self.temper = jnp.exp(jnp.full((1, 128), scal_ref[0], F32))
        self.bias = scal_ref[1]
        self.labels = label_ref
        self.place = place_ref[0]
        self.columns = {}
        self.sums = None

    def side(self):
        return 1 - 2 * lax.rem(self.place, 2)

    def label_row(self, offset):
        count = self.labels.shape[0]
        at = lax.rem(self.place + offset + count, count)
        return self.labels[pl.ds(at, 1), :]

    def label_column(self, name, offset):
        if name not in self.columns:
            self.columns[name] = as_column(self.label_row(offset).astype(F32))
        return self.columns[name]

    def grads(self, image, text, weight, image_label, text_label, count_it):
        scaled = self.temper * matmul_t(image, text)
        logit = scaled + self.bias
        pos = image_label == text_label.astype(F32)
        small = jnp.exp(-jnp.abs(logit))
        share = 1.0 / (1.0 + small)
        sigmoid = jnp.where(logit >= 0, share, small * share)
        grad = weight * (sigmoid - pos.astype(F32))
        if count_it:
            signed = jnp.where(pos, -logit, logit)
            loss = weight * (jnp.maximum(signed, 0.0) + jnp.log1p(small))
            terms = (loss, grad * scaled, grad)
            self.sums = terms if self.sums is None else tuple(a + b for a, b in zip(self.sums, terms))
        return grad.astype(BF16)

    def store_sums(self, out_ref, more_ref=None):
        out_ref[...] = jnp.zeros_like(out_ref) if more_ref is None else more_ref[...]
        for at in range(3):
            out_ref[at : at + 1, :] += jnp.sum(self.sums[at], axis=0, keepdims=True)


def weight_of(packed, width):
    parts = [packed[:, width + at : width + at + 1].astype(F32) for at in (0, 32, 64)]
    return parts[0] + parts[1] + parts[2]


def text_kernel(text_ref, text_unit_ref):
    text_unit_ref[...] = normalize(text_ref[...])[0].astype(BF16)


def image_kernel(image_ref, weight_ref, text_unit_ref, both_ref):
    width = image_ref.shape[1]
    weight = as_column(weight_ref[...])
    high = weight.astype(BF16)
    rest = weight - high.astype(F32)
    middle = rest.astype(BF16)
    low = (rest - middle.astype(F32)).astype(BF16)
    lane = lax.broadcasted_iota(jnp.int32, weight.shape, 1)
    coded = jnp.where(lane < 32, high.astype(F32), jnp.where(lane < 64, middle.astype(F32), low.astype(F32)))
    both_ref[:, :width] = normalize(image_ref[...])[0].astype(BF16)
    both_ref[:, width : width + 128] = coded.astype(BF16)
    both_ref[:, width + 128 :] = text_unit_ref[...]


def own_kernel(
    scal_ref, place_ref, label_ref, own_ref, cross_ref,
    image_total_ref, text_total_ref, cross_total_ref, sums_ref,
):
    width = cross_ref.shape[1]
    scorer = Scorer(scal_ref, label_ref, place_ref)
    u, v = own_ref[:, :width], own_ref[:, width + 128 :]
    vc = cross_ref[...]
    w = weight_of(own_ref, width)
    row = scorer.label_row(0)
    col = as_column(row.astype(F32))
    g0 = scorer.grads(u, v, w, col, row, True)
    gc = scorer.grads(u, vc, w, col, scorer.label_row(scorer.side()), True)
    image_total_ref[...] = matmul(g0, v) + matmul(gc, vc)
    text_total_ref[...] = t_matmul(g0, u)
    cross_total_ref[...] = t_matmul(gc, u)
    scorer.store_sums(sums_ref)


def early_kernel(
    scal_ref, place_ref, label_ref, own_ref, after_ref, before_ref, cross_ref,
    image_in_ref, text_in_ref, cross_in_ref, sums_in_ref,
    image_total_ref, text_total_ref, cross_total_ref, near_ref, image_far_ref, text_far_ref, sums_ref,
):
    rows, width = cross_ref.shape
    scorer = Scorer(scal_ref, label_ref, place_ref)
    side = scorer.side()
    even = side == 1
    u, v = own_ref[:, :width], own_ref[:, width + 128 :]
    ua, va = after_ref[:, :width], after_ref[:, width + 128 :]
    ub, vb = before_ref[:, :width], before_ref[:, width + 128 :]
    vc = cross_ref[...]
    w, wa, wb = weight_of(own_ref, width), weight_of(after_ref, width), weight_of(before_ref, width)
    row, row_a, row_b = scorer.label_row(0), scorer.label_row(2), scorer.label_row(-2)
    row_c = scorer.label_row(side)
    col, col_a, col_b = as_column(row.astype(F32)), as_column(row_a.astype(F32)), as_column(row_b.astype(F32))
    ux, wx, col_x = jnp.where(even, ub, ua), jnp.where(even, wb, wa), jnp.where(even, col_b, col_a)
    un, wn, col_n = jnp.where(even, ua, ub), jnp.where(even, wa, wb), jnp.where(even, col_a, col_b)
    gx = scorer.grads(ux, vc, wx, col_x, row_c, True)
    gn = scorer.grads(un, vc, wn, col_n, row_c, False)
    cross_total_ref[...] = (cross_in_ref[...] + t_matmul(gx, ux) + t_matmul(gn, un)).astype(BF16)
    ga = scorer.grads(u, va, w, col, row_a, True)
    gb = scorer.grads(u, vb, w, col, row_b, True)
    gfar = scorer.grads(ub, va, wb, col_b, row_a, True)
    ta = scorer.grads(ua, v, wa, col_a, row, False)
    tb = scorer.grads(ub, v, wb, col_b, row, False)
    image_total_ref[...] = image_in_ref[...] + matmul(ga, va) + matmul(gb, vb)
    text_total_ref[...] = text_in_ref[...] + t_matmul(ta, ua) + t_matmul(tb, ub)
    image_far, text_far = matmul(gfar, va), t_matmul(gfar, ub)
    near_ref[:rows, :] = (matmul(gx, vc) + jnp.where(even, image_far, 0.0)).astype(BF16)
    near_ref[rows:, :] = jnp.where(even, 0.0, text_far).astype(BF16)
    image_far_ref[...] = jnp.where(even, 0.0, image_far)
    text_far_ref[...] = jnp.where(even, text_far, 0.0).astype(BF16)
    scorer.store_sums(sums_ref, sums_in_ref)


def relay_kernel(
    scal_ref, place_ref, label_ref, own_ref, after_ref, before_ref, relay_ref, early_ref,
    image_in_ref, image_far_ref, text_far_ref,
    image_total_ref, far_ref, diagonal_ref, sums_ref,
):
    rows, width = relay_ref.shape
    scorer = Scorer(scal_ref, label_ref, place_ref)
    side = scorer.side()
    even = side == 1
    vr = relay_ref[...]
    row_r = scorer.label_row(-side)
    col = as_column(scorer.label_row(0).astype(F32))
    col_x = as_column(scorer.label_row(2 * side).astype(F32))
    ux = jnp.where(even, after_ref[:, :width], before_ref[:, :width])
    wx = jnp.where(even, weight_of(after_ref, width), weight_of(before_ref, width))
    gr = scorer.grads(own_ref[:, :width], vr, weight_of(own_ref, width), col, row_r, True)
    gx = scorer.grads(ux, vr, wx, col_x, row_r, True)
    lane = lax.broadcasted_iota(jnp.int32, (1, 128), 1)
    message = jnp.zeros((1, 128), F32)
    for at in range(3):
        total = jnp.sum(scorer.sums[at], axis=0, keepdims=True) + early_ref[at : at + 1, :]
        message = jnp.where(lane == at, jnp.sum(total, axis=1, keepdims=True), message)
    sums_ref[...] = message
    diagonal_ref[...] = t_matmul(gx, ux).astype(BF16)
    far_ref[:rows, :] = (image_far_ref[...] + matmul(gx, vr)).astype(BF16)
    far_ref[rows:, :] = text_far_ref[...]
    image_total_ref[...] = image_in_ref[...] + matmul(gr, vr)


def middle_kernel(
    image_in_ref, text_in_ref, near_ref, cross_ref, got_ref, image_total_ref, text_total_ref, sums_ref
):
    rows = cross_ref.shape[0]
    image_total_ref[...] = image_in_ref[...] + near_ref[:rows, :].astype(F32)
    text_total_ref[...] = text_in_ref[...] + near_ref[rows:, :].astype(F32) + cross_ref[...].astype(F32)
    sums_ref[...] = jnp.sum(got_ref[...], axis=0, keepdims=True)


def final_kernel(
    count, scal_ref, image_ref, text_ref, image_total_ref, text_total_ref, far_ref, diagonal_ref, got_ref,
    image_grad_ref, text_grad_ref, stats_ref,
):
    rows, width = image_ref.shape
    temper = jnp.exp(jnp.full((1, 128), scal_ref[0], F32))[:, :1]
    image_total = image_total_ref[...] + far_ref[:rows, :].astype(F32)
    text_total = text_total_ref[...] + far_ref[rows:, :].astype(F32) + diagonal_ref[...].astype(F32)
    for raw_ref, total, out_ref in ((image_ref, image_total, image_grad_ref), (text_ref, text_total, text_grad_ref)):
        unit, scale = normalize(raw_ref[...])
        out_ref[...] = norm_back(unit, scale, temper * total).astype(BF16)
    got = jnp.sum(got_ref[...], axis=0, keepdims=True) / count
    for at in range(3):
        stats_ref[at] = got[0, at]


def call(kernel, ins, outs, name, work, out_specs=None):
    return pl.pallas_call(
        kernel,
        out_shape=outs,
        in_specs=ins,
        out_specs=jax.tree.map(lambda _: VMEM, outs) if out_specs is None else out_specs,
        compiler_params=PARAMS,
        cost_estimate=pl.CostEstimate(flops=work, bytes_accessed=0, transcendentals=0),
        name=name,
    )


def exchanged(row, axis):
    count = lax.axis_size(axis)
    sent = jnp.broadcast_to(row.reshape(1, 1, 128), (count, 1, 128))
    return lax.all_to_all(sent, axis, 0, 0).reshape(count, 128)


def per_device(images, texts, labels, weights, log_temp, bias):
    cycle = lax.axis_size("blk")
    groups = lax.axis_size("group")
    rows, width = images.shape
    place = lax.axis_index("blk").astype(jnp.int32).reshape(1)
    scal = jnp.concatenate([log_temp, bias])
    head = [SMEM, SMEM, VMEM]
    dot = 2 * rows * rows * width

    def passed(value, step_of):
        return lax.ppermute(value, "blk", [(p, (p + step_of(p)) % cycle) for p in range(cycle)])

    def across(value):
        return passed(value, lambda p: 1 - 2 * (p % 2))

    def diagonally(value):
        return passed(value, lambda p: 2 * (p % 2) - 1)

    def far_side(value):
        return passed(value, lambda p: 2 - 4 * (p % 2))

    def near_side(value):
        return passed(value, lambda p: 4 * (p % 2) - 2)

    def upward(value):
        return passed(value, lambda p: 2)

    def downward(value):
        return passed(value, lambda p: -2)

    block, half = shape(rows, width, F32), shape(rows, width, BF16)
    text_unit = call(text_kernel, [VMEM], half, "text", 10 * dot)(texts)
    cross_v = across(text_unit)
    both = call(image_kernel, [VMEM] * 3, shape(rows, 2 * width + 128, BF16), "image", 10 * dot)(
        images, weights.reshape(1, rows), text_unit
    )
    after = downward(both)
    before = upward(both)
    relay_v = far_side(cross_v)
    image_total, text_total, cross_total, sums = call(
        own_kernel, head + [VMEM] * 2, (block,) * 3 + (shape(8, 128, F32),), "own", 200 * dot
    )(scal, place, labels, both, cross_v)
    pair = shape(2 * rows, width, BF16)
    image_total, text_total, cross_total, near, image_far, text_far, sums = call(
        early_kernel,
        head + [VMEM] * 8,
        (block, block, half, pair, block, half, shape(8, 128, F32)),
        "early",
        20 * dot,
    )(scal, place, labels, both, after, before, cross_v, image_total, text_total, cross_total, sums)
    from_cross = across(cross_total)
    from_near = near_side(near)
    image_total, far, diagonal, sums = call(
        relay_kernel, head + [VMEM] * 8, (block, pair, half, shape(1, 128, F32)), "relay", 10 * dot
    )(scal, place, labels, both, after, before, relay_v, sums, image_total, image_far, text_far)
    from_diagonal = diagonally(diagonal)
    from_far = far_side(far)
    got = exchanged(sums, "group")
    image_total, text_total, sums = call(
        middle_kernel, [VMEM] * 5, (block, block, shape(1, 128, F32)), "middle", 10 * dot
    )(image_total, text_total, from_near, from_cross, got)
    got = exchanged(sums, "blk")
    count = float(cycle * groups * rows) * float(rows) * 8.0
    image_grad, text_grad, stats = call(
        functools.partial(final_kernel, count),
        [SMEM] + [VMEM] * 7,
        (half, half, jax.ShapeDtypeStruct((3,), F32)),
        "final",
        10 * dot,
        (VMEM, VMEM, SMEM),
    )(scal, images, texts, image_total, text_total, from_far, from_diagonal, got)
    return image_grad, text_grad, stats


def solution(mesh):
    rows = P(("blk", "group"), None)
    in_specs = (rows, rows, P(None, "group"), P(("blk", "group")), P(), P())
    return jax.shard_map(per_device, mesh=mesh, in_specs=in_specs, out_specs=(rows, rows, P()), check_vma=False)
```

```python
import functools

import jax
import jax.numpy as jnp
from jax import lax
from jax.experimental import pallas as pl
from jax.experimental.pallas import tpu as pltpu
from jax.sharding import PartitionSpec as P

VMEM = pl.BlockSpec(memory_space=pltpu.VMEM)
SMEM = pl.BlockSpec(memory_space=pltpu.SMEM)
F32 = jnp.float32
BF16 = jnp.bfloat16
PARAMS = pltpu.CompilerParams(vmem_limit_bytes=16 * 1024 * 1024)


def shape(rows, cols, dtype):
    return jax.ShapeDtypeStruct((rows, cols), dtype)


def as_column(row):
    n = row.shape[1]
    return jnp.broadcast_to(row, (n, n)).T


def normalize(raw):
    values = raw.astype(F32)
    scale = lax.rsqrt(jnp.sum(values * values, axis=-1, keepdims=True) + 1e-06)
    return values * scale, scale


def norm_back(unit, scale, upstream):
    return (upstream - unit * jnp.sum(unit * upstream, axis=-1, keepdims=True)) * scale


def matmul_t(a, b):
    return lax.dot_general(a, b, (((1,), (1,)), ((), ())), preferred_element_type=F32)


def matmul(a, b):
    return jnp.dot(a, b, preferred_element_type=F32)


def t_matmul(a, b):
    return lax.dot_general(a, b, (((0,), (0,)), ((), ())), preferred_element_type=F32)


class Scorer:
    def __init__(self, scal_ref, label_ref, place_ref):
        self.temper = jnp.exp(jnp.full((1, 128), scal_ref[0], F32))
        self.bias = scal_ref[1]
        self.labels = label_ref
        self.place = place_ref[0]
        self.columns = {}
        self.sums = None

    def side(self):
        return 1 - 2 * lax.rem(self.place, 2)

    def label_row(self, offset):
        count = self.labels.shape[0]
        at = lax.rem(self.place + offset + count, count)
        return self.labels[pl.ds(at, 1), :]

    def label_column(self, name, offset):
        if name not in self.columns:
            self.columns[name] = as_column(self.label_row(offset).astype(F32))
        return self.columns[name]

    def grads(self, image, text, weight, image_label, text_label, count_it):
        scaled = self.temper * matmul_t(image, text)
        logit = scaled + self.bias
        pos = image_label == text_label.astype(F32)
        small = jnp.exp(-jnp.abs(logit))
        share = 1.0 / (1.0 + small)
        sigmoid = jnp.where(logit >= 0, share, small * share)
        grad = weight * (sigmoid - pos.astype(F32))
        if count_it:
            signed = jnp.where(pos, -logit, logit)
            loss = weight * (jnp.maximum(signed, 0.0) + jnp.log1p(small))
            terms = (loss, grad * scaled, grad)
            self.sums = terms if self.sums is None else tuple(a + b for a, b in zip(self.sums, terms))
        return grad.astype(BF16)

    def store_sums(self, out_ref, more_ref=None):
        out_ref[...] = jnp.zeros_like(out_ref) if more_ref is None else more_ref[...]
        for at in range(3):
            out_ref[at : at + 1, :] += jnp.sum(self.sums[at], axis=0, keepdims=True)


def weight_of(packed, width):
    parts = [packed[:, width + at : width + at + 1].astype(F32) for at in (0, 32, 64)]
    return parts[0] + parts[1] + parts[2]


def text_kernel(text_ref, text_unit_ref):
    text_unit_ref[...] = normalize(text_ref[...])[0].astype(BF16)


def image_kernel(image_ref, weight_ref, text_unit_ref, image_pack_ref, both_ref):
    width = image_ref.shape[1]
    u = normalize(image_ref[...])[0].astype(BF16)
    weight = as_column(weight_ref[...])
    high = weight.astype(BF16)
    rest = weight - high.astype(F32)
    middle = rest.astype(BF16)
    low = (rest - middle.astype(F32)).astype(BF16)
    lane = lax.broadcasted_iota(jnp.int32, weight.shape, 1)
    coded = jnp.where(lane < 32, high.astype(F32), jnp.where(lane < 64, middle.astype(F32), low.astype(F32))).astype(BF16)
    image_pack_ref[:, :width] = u
    image_pack_ref[:, width:] = coded
    both_ref[:, :width] = u
    both_ref[:, width : width + 128] = coded
    both_ref[:, width + 128 :] = text_unit_ref[...]


def own_kernel(scal_ref, place_ref, label_ref, own_ref, cross_ref, image_total_ref, text_total_ref, sums_ref):
    width = cross_ref.shape[1]
    scorer = Scorer(scal_ref, label_ref, place_ref)
    u, v = own_ref[:, :width], own_ref[:, width + 128 :]
    vc = cross_ref[...]
    w = weight_of(own_ref, width)
    row = scorer.label_row(0)
    col = as_column(row.astype(F32))
    g0 = scorer.grads(u, v, w, col, row, True)
    gc = scorer.grads(u, vc, w, col, scorer.label_row(scorer.side()), True)
    image_total_ref[...] = matmul(g0, v) + matmul(gc, vc)
    text_total_ref[...] = t_matmul(g0, u)
    scorer.store_sums(sums_ref)


def early_kernel(
    scal_ref, place_ref, label_ref, own_ref, after_ref, before_ref, cross_ref,
    image_in_ref, text_in_ref, sums_in_ref,
    image_total_ref, text_total_ref, far_ref, down_ref, up_ref, sums_ref,
):
    width = cross_ref.shape[1]
    scorer = Scorer(scal_ref, label_ref, place_ref)
    side = scorer.side()
    even = side == 1
    u, v = own_ref[:, :width], own_ref[:, width + 128 :]
    ua, va = after_ref[:, :width], after_ref[:, width + 128 :]
    ub, vb = before_ref[:, :width], before_ref[:, width + 128 :]
    vc = cross_ref[...]
    w, wa, wb = weight_of(own_ref, width), weight_of(after_ref, width), weight_of(before_ref, width)
    row, row_a, row_b = scorer.label_row(0), scorer.label_row(2), scorer.label_row(-2)
    row_c = scorer.label_row(side)
    col, col_a, col_b = as_column(row.astype(F32)), as_column(row_a.astype(F32)), as_column(row_b.astype(F32))
    ga = scorer.grads(u, va, w, col, row_a, True)
    gb = scorer.grads(u, vb, w, col, row_b, True)
    gfar = scorer.grads(ub, va, wb, col_b, row_a, True)
    ux = jnp.where(even, ub, ua)
    gx = scorer.grads(ux, vc, jnp.where(even, wb, wa), jnp.where(even, col_b, col_a), row_c, True)
    ta = scorer.grads(ua, v, wa, col_a, row, False)
    tb = scorer.grads(ub, v, wb, col_b, row, False)
    image_total_ref[...] = image_in_ref[...] + matmul(ga, va) + matmul(gb, vb)
    text_total_ref[...] = text_in_ref[...] + t_matmul(ta, ua) + t_matmul(tb, ub)
    far_ref[...] = matmul(gx, vc)
    down_ref[...] = matmul(gfar, va)
    up_ref[...] = t_matmul(gfar, ub)
    scorer.store_sums(sums_ref, sums_in_ref)


def relay_kernel(
    scal_ref, place_ref, label_ref, own_ref, after_ref, before_ref, relay_ref, early_ref,
    near_ref, far_ref, sums_ref,
):
    width = relay_ref.shape[1]
    scorer = Scorer(scal_ref, label_ref, place_ref)
    side = scorer.side()
    even = side == 1
    vr = relay_ref[...]
    row_r = scorer.label_row(-side)
    col = as_column(scorer.label_row(0).astype(F32))
    col_x = as_column(scorer.label_row(2 * side).astype(F32))
    near_ref[...] = scorer.grads(own_ref[:, :width], vr, weight_of(own_ref, width), col, row_r, True)
    ux = jnp.where(even, after_ref[:, :width], before_ref[:, :width])
    wx = jnp.where(even, weight_of(after_ref, width), weight_of(before_ref, width))
    far_ref[...] = scorer.grads(ux, vr, wx, col_x, row_r, True)
    lane = lax.broadcasted_iota(jnp.int32, (1, 128), 1)
    message = jnp.zeros((1, 128), F32)
    for at in range(3):
        total = jnp.sum(scorer.sums[at], axis=0, keepdims=True) + early_ref[at : at + 1, :]
        message = jnp.where(lane == at, jnp.sum(total, axis=1, keepdims=True), message)
    sums_ref[...] = message


def late_kernel(
    scal_ref, place_ref, label_ref, own_ref, after_ref, before_ref, cross_ref, relay_ref, relay_v_ref,
    near_ref, far_g_ref, far_ref, down_in_ref, up_in_ref, image_in_ref, text_in_ref,
    up_ref, down_ref, image_total_ref, text_total_ref,
):
    width = relay_v_ref.shape[1]
    rows = relay_v_ref.shape[0]
    scorer = Scorer(scal_ref, label_ref, place_ref)
    side = scorer.side()
    even = side == 1
    v = own_ref[:, width + 128 :]
    va, vb = after_ref[:, width + 128 :], before_ref[:, width + 128 :]
    uc, ur = cross_ref[:, :width], relay_ref[:, :width]
    wc, wr = weight_of(cross_ref, width), weight_of(relay_ref, width)
    col_c = as_column(scorer.label_row(side).astype(F32))
    col_r = as_column(scorer.label_row(-side).astype(F32))
    row, row_a, row_b = scorer.label_row(0), scorer.label_row(2), scorer.label_row(-2)
    gcx = scorer.grads(uc, jnp.where(even, vb, va), wc, col_c, jnp.where(even, row_b, row_a), False)
    grx = scorer.grads(ur, jnp.where(even, va, vb), wr, col_r, jnp.where(even, row_a, row_b), False)
    far_text_c = t_matmul(gcx, uc)
    far_text_r = t_matmul(grx, ur)
    far_image_c = far_ref[...]
    far_image_r = matmul(far_g_ref[...], relay_v_ref[...])
    up_ref[:rows, :] = jnp.where(even, far_image_r, far_image_c).astype(BF16)
    up_ref[rows:, :] = (up_in_ref[...] + jnp.where(even, far_text_r, far_text_c)).astype(BF16)
    down_ref[:rows, :] = (down_in_ref[...] + jnp.where(even, far_image_c, far_image_r)).astype(BF16)
    down_ref[rows:, :] = jnp.where(even, far_text_c, far_text_r).astype(BF16)
    gc = scorer.grads(uc, v, wc, col_c, row, False)
    gr = scorer.grads(ur, v, wr, col_r, row, False)
    image_total_ref[...] = image_in_ref[...] + matmul(near_ref[...], relay_v_ref[...])
    text_total_ref[...] = text_in_ref[...] + t_matmul(gc, uc) + t_matmul(gr, ur)


def middle_kernel(got_ref, sums_ref):
    sums_ref[...] = jnp.sum(got_ref[...], axis=0, keepdims=True)


def final_kernel(
    count, scal_ref, image_ref, text_ref, image_total_ref, text_total_ref, up_ref, down_ref, got_ref,
    image_grad_ref, text_grad_ref, stats_ref,
):
    rows, width = image_ref.shape
    temper = jnp.exp(jnp.full((1, 128), scal_ref[0], F32))[:, :1]
    for raw_ref, total_ref, out_ref, at in (
        (image_ref, image_total_ref, image_grad_ref, 0),
        (text_ref, text_total_ref, text_grad_ref, rows),
    ):
        total = total_ref[...] + up_ref[at : at + rows, :].astype(F32) + down_ref[at : at + rows, :].astype(F32)
        unit, scale = normalize(raw_ref[...])
        out_ref[...] = norm_back(unit, scale, temper * total).astype(BF16)
    got = jnp.sum(got_ref[...], axis=0, keepdims=True) / count
    for at in range(3):
        stats_ref[at] = got[0, at]


def call(kernel, ins, outs, name, work, out_specs=None):
    return pl.pallas_call(
        kernel,
        out_shape=outs,
        in_specs=ins,
        out_specs=jax.tree.map(lambda _: VMEM, outs) if out_specs is None else out_specs,
        compiler_params=PARAMS,
        cost_estimate=pl.CostEstimate(flops=work, bytes_accessed=0, transcendentals=0),
        name=name,
    )


def exchanged(row, axis):
    count = lax.axis_size(axis)
    sent = jnp.broadcast_to(row.reshape(1, 1, 128), (count, 1, 128))
    return lax.all_to_all(sent, axis, 0, 0).reshape(count, 128)


def per_device(images, texts, labels, weights, log_temp, bias):
    cycle = lax.axis_size("blk")
    groups = lax.axis_size("group")
    rows, width = images.shape
    place = lax.axis_index("blk").astype(jnp.int32).reshape(1)
    scal = jnp.concatenate([log_temp, bias])
    head = [SMEM, SMEM, VMEM]
    dot = 2 * rows * rows * width

    def passed(value, step_of):
        return lax.ppermute(value, "blk", [(p, (p + step_of(p)) % cycle) for p in range(cycle)])

    def across(value):
        return passed(value, lambda p: 1 - 2 * (p % 2))

    def relayed(value):
        return passed(value, lambda p: 2 - 4 * (p % 2))

    def upward(value):
        return passed(value, lambda p: 2)

    def downward(value):
        return passed(value, lambda p: -2)

    block = shape(rows, width, F32)
    text_unit = call(text_kernel, [VMEM], shape(rows, width, BF16), "text", 10 * dot)(texts)
    cross_v = across(text_unit)
    image_pack, both = call(
        image_kernel,
        [VMEM] * 3,
        (shape(rows, width + 128, BF16), shape(rows, 2 * width + 128, BF16)),
        "image",
        10 * dot,
    )(images, weights.reshape(1, rows), text_unit)
    after = downward(both)
    before = upward(both)
    cross_u = across(image_pack)
    relay_v = relayed(cross_v)
    image_total, text_total, sums = call(
        own_kernel, head + [VMEM] * 2, (block,) * 2 + (shape(8, 128, F32),), "own", 150 * dot
    )(scal, place, labels, both, cross_v)
    image_total, text_total, far, far_down, far_up, sums = call(
        early_kernel, head + [VMEM] * 7, (block,) * 5 + (shape(8, 128, F32),), "early", 20 * dot
    )(scal, place, labels, both, after, before, cross_v, image_total, text_total, sums)
    cross_u, sums = lax.optimization_barrier((cross_u, sums))
    relay_u = relayed(cross_u)
    near_g, far_g, sums = call(
        relay_kernel, head + [VMEM] * 5, (shape(rows, rows, BF16),) * 2 + (shape(1, 128, F32),), "relay", 10 * dot
    )(scal, place, labels, both, after, before, relay_v, sums)
    got = exchanged(sums, "group")
    to_up, to_down, image_total, text_total = call(
        late_kernel,
        head + [VMEM] * 13,
        (shape(2 * rows, width, BF16),) * 2 + (block,) * 2,
        "late",
        400 * dot,
    )(
        scal, place, labels, both, after, before, cross_u, relay_u, relay_v,
        near_g, far_g, far, far_down, far_up, image_total, text_total,
    )
    from_below = upward(to_up)
    from_above = downward(to_down)
    sums = call(middle_kernel, [VMEM], shape(1, 128, F32), "middle", 300 * dot)(got)
    got = exchanged(sums, "blk")
    count = float(cycle * groups * rows) * float(rows) * 8.0
    image_grad, text_grad, stats = call(
        functools.partial(final_kernel, count),
        [SMEM] + [VMEM] * 7,
        (shape(rows, width, BF16),) * 2 + (jax.ShapeDtypeStruct((3,), F32),),
        "final",
        10 * dot,
        (VMEM, VMEM, SMEM),
    )(scal, images, texts, image_total, text_total, from_below, from_above, got)
    return image_grad, text_grad, stats


def solution(mesh):
    rows = P(("blk", "group"), None)
    in_specs = (rows, rows, P(None, "group"), P(("blk", "group")), P(), P())
    return jax.shard_map(per_device, mesh=mesh, in_specs=in_specs, out_specs=(rows, rows, P()), check_vma=False)
```

```python
import functools

import jax
import jax.numpy as jnp
from jax import lax
from jax.experimental import pallas as pl
from jax.experimental.pallas import tpu as pltpu
from jax.sharding import PartitionSpec as P

VMEM = pl.BlockSpec(memory_space=pltpu.VMEM)
SMEM = pl.BlockSpec(memory_space=pltpu.SMEM)
F32 = jnp.float32
BF16 = jnp.bfloat16
HBM = pl.BlockSpec(memory_space=pltpu.HBM)
PARAMS = pltpu.CompilerParams(vmem_limit_bytes=16 * 1024 * 1024)


def shape(rows, cols, dtype):
    return jax.ShapeDtypeStruct((rows, cols), dtype)


def as_column(row):
    n = row.shape[1]
    return jnp.broadcast_to(row, (n, n)).T


def normalize(raw):
    values = raw.astype(F32)
    scale = lax.rsqrt(jnp.sum(values * values, axis=-1, keepdims=True) + 1e-06)
    return values * scale, scale


def norm_back(unit, scale, upstream):
    return (upstream - unit * jnp.sum(unit * upstream, axis=-1, keepdims=True)) * scale


def matmul_t(a, b):
    return lax.dot_general(a, b, (((1,), (1,)), ((), ())), preferred_element_type=F32)


def matmul(a, b):
    return jnp.dot(a, b, preferred_element_type=F32)


def t_matmul(a, b):
    return lax.dot_general(a, b, (((0,), (0,)), ((), ())), preferred_element_type=F32)


class Scorer:
    def __init__(self, scal_ref, label_ref, place_ref):
        self.temper = jnp.exp(jnp.full((1, 128), scal_ref[0], F32))
        self.bias = scal_ref[1]
        self.labels = label_ref
        self.place = place_ref[0]
        self.columns = {}
        self.sums = None

    def side(self):
        return 1 - 2 * lax.rem(self.place, 2)

    def label_row(self, offset):
        count = self.labels.shape[0]
        at = lax.rem(self.place + offset + count, count)
        return self.labels[pl.ds(at, 1), :]

    def label_column(self, name, offset):
        if name not in self.columns:
            self.columns[name] = as_column(self.label_row(offset).astype(F32))
        return self.columns[name]

    def grads(self, image, text, weight, image_label, text_label, count_it):
        scaled = self.temper * matmul_t(image, text)
        logit = scaled + self.bias
        pos = image_label == text_label.astype(F32)
        small = jnp.exp(-jnp.abs(logit))
        share = 1.0 / (1.0 + small)
        sigmoid = jnp.where(logit >= 0, share, small * share)
        grad = weight * (sigmoid - pos.astype(F32))
        if count_it:
            signed = jnp.where(pos, -logit, logit)
            loss = weight * (jnp.maximum(signed, 0.0) + jnp.log1p(small))
            terms = (loss, grad * scaled, grad)
            self.sums = terms if self.sums is None else tuple(a + b for a, b in zip(self.sums, terms))
        return grad.astype(BF16)

    def store_sums(self, out_ref, more_ref=None):
        out_ref[...] = jnp.zeros_like(out_ref) if more_ref is None else more_ref[...]
        for at in range(3):
            out_ref[at : at + 1, :] += jnp.sum(self.sums[at], axis=0, keepdims=True)


def weight_of(packed, width):
    parts = [packed[:, width + at : width + at + 1].astype(F32) for at in (0, 32, 64)]
    return parts[0] + parts[1] + parts[2]


def text_kernel(text_ref, text_unit_ref):
    text_unit_ref[...] = normalize(text_ref[...])[0].astype(BF16)


def image_kernel(image_ref, weight_ref, text_unit_ref, image_pack_ref, both_ref):
    width = image_ref.shape[1]
    u = normalize(image_ref[...])[0].astype(BF16)
    weight = as_column(weight_ref[...])
    high = weight.astype(BF16)
    rest = weight - high.astype(F32)
    middle = rest.astype(BF16)
    low = (rest - middle.astype(F32)).astype(BF16)
    lane = lax.broadcasted_iota(jnp.int32, weight.shape, 1)
    coded = jnp.where(lane < 32, high.astype(F32), jnp.where(lane < 64, middle.astype(F32), low.astype(F32))).astype(BF16)
    image_pack_ref[:, :width] = u
    image_pack_ref[:, width:] = coded
    both_ref[:, :width] = u
    both_ref[:, width : width + 128] = coded
    both_ref[:, width + 128 :] = text_unit_ref[...]


def own_kernel(scal_ref, place_ref, label_ref, own_ref, cross_ref, image_total_ref, text_total_ref, sums_ref):
    width = cross_ref.shape[1]
    scorer = Scorer(scal_ref, label_ref, place_ref)
    u, v = own_ref[:, :width], own_ref[:, width + 128 :]
    vc = cross_ref[...]
    w = weight_of(own_ref, width)
    row = scorer.label_row(0)
    col = as_column(row.astype(F32))
    g0 = scorer.grads(u, v, w, col, row, True)
    gc = scorer.grads(u, vc, w, col, scorer.label_row(scorer.side()), True)
    image_total_ref[...] = matmul(g0, v) + matmul(gc, vc)
    text_total_ref[...] = t_matmul(g0, u)
    scorer.store_sums(sums_ref)


def early_kernel(
    scal_ref, place_ref, label_ref, own_ref, after_ref, before_ref, cross_ref,
    image_in_ref, text_in_ref, sums_in_ref,
    image_total_ref, text_total_ref, far_g_ref, sums_ref,
):
    rows, width = cross_ref.shape
    scorer = Scorer(scal_ref, label_ref, place_ref)
    side = scorer.side()
    even = side == 1
    u, v = own_ref[:, :width], own_ref[:, width + 128 :]
    ua, va = after_ref[:, :width], after_ref[:, width + 128 :]
    ub, vb = before_ref[:, :width], before_ref[:, width + 128 :]
    vc = cross_ref[...]
    w, wa, wb = weight_of(own_ref, width), weight_of(after_ref, width), weight_of(before_ref, width)
    row, row_a, row_b = scorer.label_row(0), scorer.label_row(2), scorer.label_row(-2)
    row_c = scorer.label_row(side)
    col, col_a, col_b = as_column(row.astype(F32)), as_column(row_a.astype(F32)), as_column(row_b.astype(F32))
    ga = scorer.grads(u, va, w, col, row_a, True)
    gb = scorer.grads(u, vb, w, col, row_b, True)
    gfar = scorer.grads(ub, va, wb, col_b, row_a, True)
    ux = jnp.where(even, ub, ua)
    gx = scorer.grads(ux, vc, jnp.where(even, wb, wa), jnp.where(even, col_b, col_a), row_c, True)
    ta = scorer.grads(ua, v, wa, col_a, row, False)
    tb = scorer.grads(ub, v, wb, col_b, row, False)
    image_total_ref[...] = image_in_ref[...] + matmul(ga, va) + matmul(gb, vb)
    text_total_ref[...] = text_in_ref[...] + t_matmul(ta, ua) + t_matmul(tb, ub)
    far_g_ref[:rows, :] = gx
    far_g_ref[rows:, :] = gfar
    scorer.store_sums(sums_ref, sums_in_ref)


def relay_kernel(
    scal_ref, place_ref, label_ref, own_ref, after_ref, before_ref, relay_ref, early_ref, far_in_ref,
    near_ref, far_ref, sums_ref,
):
    width = relay_ref.shape[1]
    scorer = Scorer(scal_ref, label_ref, place_ref)
    side = scorer.side()
    even = side == 1
    vr = relay_ref[...]
    row_r = scorer.label_row(-side)
    col = as_column(scorer.label_row(0).astype(F32))
    col_x = as_column(scorer.label_row(2 * side).astype(F32))
    near_ref[...] = scorer.grads(own_ref[:, :width], vr, weight_of(own_ref, width), col, row_r, True)
    ux = jnp.where(even, after_ref[:, :width], before_ref[:, :width])
    wx = jnp.where(even, weight_of(after_ref, width), weight_of(before_ref, width))
    rows = relay_ref.shape[0]
    far_ref[:rows, :] = scorer.grads(ux, vr, wx, col_x, row_r, True)
    far_ref[rows:, :] = far_in_ref[...]
    lane = lax.broadcasted_iota(jnp.int32, (1, 128), 1)
    message = jnp.zeros((1, 128), F32)
    for at in range(3):
        total = jnp.sum(scorer.sums[at], axis=0, keepdims=True) + early_ref[at : at + 1, :]
        message = jnp.where(lane == at, jnp.sum(total, axis=1, keepdims=True), message)
    sums_ref[...] = message


def late_kernel(
    scal_ref, place_ref, label_any, own_any, after_any, before_any, cross_any, relay_any, relay_v_any,
    far_g_any, cross_v_any,
    to_up_ref, to_down_ref, cross_g_ref, relay_g_ref,
    label_ref, v_ref, va_ref, before_ref, cross_ref, relay_ref, relay_v_ref, far_g_ref, cross_v_ref,
    sems,
):
    rows, width = relay_v_ref.shape
    text_part = (slice(None), pl.ds(width + 128, width))
    copies = [
        pltpu.make_async_copy(source, target, sems.at[at])
        for at, (source, target) in enumerate((
            (label_any, label_ref),
            (cross_any, cross_ref),
            (before_any, before_ref),
            (after_any.at[text_part], va_ref),
            (own_any.at[text_part], v_ref),
            (relay_any, relay_ref),
            (far_g_any, far_g_ref),
            (relay_v_any, relay_v_ref),
            (cross_v_any, cross_v_ref),
        ))
    ]
    for copy in copies:
        copy.start()
    for copy in copies[:5]:
        copy.wait()
    scorer = Scorer(scal_ref, label_ref, place_ref)
    side = scorer.side()
    even = side == 1
    v, va, vb = v_ref[...], va_ref[...], before_ref[:, width + 128 :]
    uc = cross_ref[:, :width]
    wc = weight_of(cross_ref, width)
    col_c = as_column(scorer.label_row(side).astype(F32))
    col_r = as_column(scorer.label_row(-side).astype(F32))
    row, row_a, row_b = scorer.label_row(0), scorer.label_row(2), scorer.label_row(-2)
    gcx = scorer.grads(uc, jnp.where(even, vb, va), wc, col_c, jnp.where(even, row_b, row_a), False)
    gc = scorer.grads(uc, v, wc, col_c, row, False)
    for copy in copies[5:]:
        copy.wait()
    ur, wr = relay_ref[:, :width], weight_of(relay_ref, width)
    grx = scorer.grads(ur, jnp.where(even, va, vb), wr, col_r, jnp.where(even, row_a, row_b), False)
    gr = scorer.grads(ur, v, wr, col_r, row, False)
    far_text_c, far_text_r = t_matmul(gcx, uc), t_matmul(grx, ur)
    far_image_r = matmul(far_g_ref[:rows, :], relay_v_ref[...])
    far_image_c = matmul(far_g_ref[rows : 2 * rows, :], cross_v_ref[...])
    g = far_g_ref[2 * rows :, :]
    to_up_ref[:rows, :] = jnp.where(even, far_image_r, far_image_c).astype(BF16)
    to_up_ref[rows:, :] = (t_matmul(g, before_ref[:, :width]) + jnp.where(even, far_text_r, far_text_c)).astype(BF16)
    to_down_ref[:rows, :] = (matmul(g, va) + jnp.where(even, far_image_c, far_image_r)).astype(BF16)
    to_down_ref[rows:, :] = jnp.where(even, far_text_c, far_text_r).astype(BF16)
    cross_g_ref[...], relay_g_ref[...] = gc, gr


def middle_kernel(got_ref, sums_ref):
    sums_ref[...] = jnp.sum(got_ref[...], axis=0, keepdims=True)


def final_kernel(
    count, scal_ref, image_ref, text_ref, image_total_ref, text_total_ref, near_g_ref, relay_v_ref,
    cross_g_ref, cross_ref, relay_g_ref, relay_ref, up_ref, down_ref, got_ref,
    image_grad_ref, text_grad_ref, stats_ref,
):
    rows, width = image_ref.shape
    temper = jnp.exp(jnp.full((1, 128), scal_ref[0], F32))[:, :1]
    image_more = matmul(near_g_ref[...], relay_v_ref[...])
    text_more = t_matmul(cross_g_ref[...], cross_ref[:, :width]) + t_matmul(relay_g_ref[...], relay_ref[:, :width])
    for raw_ref, total_ref, more, out_ref, at in (
        (image_ref, image_total_ref, image_more, image_grad_ref, 0),
        (text_ref, text_total_ref, text_more, text_grad_ref, rows),
    ):
        total = total_ref[...] + more + up_ref[at : at + rows, :].astype(F32) + down_ref[at : at + rows, :].astype(F32)
        unit, scale = normalize(raw_ref[...])
        out_ref[...] = norm_back(unit, scale, temper * total).astype(BF16)
    got = jnp.sum(got_ref[...], axis=0, keepdims=True) / count
    for at in range(3):
        stats_ref[at] = got[0, at]


def call(kernel, ins, outs, name, work, out_specs=None, scratch=()):
    return pl.pallas_call(
        kernel,
        out_shape=outs,
        in_specs=ins,
        out_specs=jax.tree.map(lambda _: VMEM, outs) if out_specs is None else out_specs,
        scratch_shapes=scratch,
        compiler_params=PARAMS,
        cost_estimate=pl.CostEstimate(flops=work, bytes_accessed=0, transcendentals=0),
        name=name,
    )


def exchanged(row, axis):
    count = lax.axis_size(axis)
    sent = jnp.broadcast_to(row.reshape(1, 1, 128), (count, 1, 128))
    return lax.all_to_all(sent, axis, 0, 0).reshape(count, 128)


def per_device(images, texts, labels, weights, log_temp, bias):
    cycle = lax.axis_size("blk")
    groups = lax.axis_size("group")
    rows, width = images.shape
    place = lax.axis_index("blk").astype(jnp.int32).reshape(1)
    scal = jnp.concatenate([log_temp, bias])
    head = [SMEM, SMEM, VMEM]
    dot = 2 * rows * rows * width

    def passed(value, step_of):
        return lax.ppermute(value, "blk", [(p, (p + step_of(p)) % cycle) for p in range(cycle)])

    def across(value):
        return passed(value, lambda p: 1 - 2 * (p % 2))

    def relayed(value):
        return passed(value, lambda p: 2 - 4 * (p % 2))

    def upward(value):
        return passed(value, lambda p: 2)

    def downward(value):
        return passed(value, lambda p: -2)

    block = shape(rows, width, F32)
    text_unit = call(text_kernel, [VMEM], shape(rows, width, BF16), "text", 10 * dot)(texts)
    cross_v = across(text_unit)
    image_pack, both = call(
        image_kernel,
        [VMEM] * 3,
        (shape(rows, width + 128, BF16), shape(rows, 2 * width + 128, BF16)),
        "image",
        10 * dot,
    )(images, weights.reshape(1, rows), text_unit)
    after = downward(both)
    before = upward(both)
    cross_u = across(image_pack)
    relay_v = relayed(cross_v)
    image_total, text_total, sums = call(
        own_kernel, head + [VMEM] * 2, (block,) * 2 + (shape(8, 128, F32),), "own", 150 * dot
    )(scal, place, labels, both, cross_v)
    image_total, text_total, far_g, sums = call(
        early_kernel, head + [VMEM] * 7, (block, block, shape(2 * rows, rows, BF16), shape(8, 128, F32)), "early", 20 * dot
    )(scal, place, labels, both, after, before, cross_v, image_total, text_total, sums)
    cross_u, sums = lax.optimization_barrier((cross_u, sums))
    relay_u = relayed(cross_u)
    near_g, far_g, sums = call(
        relay_kernel,
        head + [VMEM] * 6,
        (shape(rows, rows, BF16), shape(3 * rows, rows, BF16), shape(1, 128, F32)),
        "relay", 10 * dot
    )(scal, place, labels, both, after, before, relay_v, sums, far_g)
    got = exchanged(sums, "group")
    half, pack = pltpu.VMEM((rows, width), BF16), pltpu.VMEM((rows, width + 128), BF16)
    scratch = [pltpu.VMEM(labels.shape, jnp.int32), half, half, pltpu.VMEM(both.shape, BF16), pack, pack, half]
    scratch += [pltpu.VMEM((3 * rows, rows), BF16), half]
    to_up, to_down, cross_g, relay_g = call(
        late_kernel,
        [SMEM, SMEM] + [HBM] * 9,
        (shape(2 * rows, width, BF16),) * 2 + (shape(rows, rows, BF16),) * 2,
        "late",
        400 * dot,
        scratch=scratch + [pltpu.SemaphoreType.DMA((9,))],
    )(scal, place, labels, both, after, before, cross_u, relay_u, relay_v, far_g, cross_v)
    from_below = upward(to_up)
    from_above = downward(to_down)
    sums = call(middle_kernel, [VMEM], shape(1, 128, F32), "middle", 300 * dot)(got)
    got = exchanged(sums, "blk")
    count = float(cycle * groups * rows) * float(rows) * 8.0
    image_grad, text_grad, stats = call(
        functools.partial(final_kernel, count),
        [SMEM] + [VMEM] * 13,
        (shape(rows, width, BF16),) * 2 + (jax.ShapeDtypeStruct((3,), F32),),
        "final",
        10 * dot,
        (VMEM, VMEM, SMEM),
    )(
        scal, images, texts, image_total, text_total, near_g, relay_v, cross_g, cross_u, relay_g, relay_u,
        from_below, from_above, got,
    )
    return image_grad, text_grad, stats


def solution(mesh):
    rows = P(("blk", "group"), None)
    in_specs = (rows, rows, P(None, "group"), P(("blk", "group")), P(), P())
    return jax.shard_map(per_device, mesh=mesh, in_specs=in_specs, out_specs=(rows, rows, P()), check_vma=False)
```

```python
import functools

import jax
import jax.numpy as jnp
from jax import lax
from jax.experimental import pallas as pl
from jax.experimental.pallas import tpu as pltpu
from jax.sharding import PartitionSpec as P

VMEM = pl.BlockSpec(memory_space=pltpu.VMEM)
SMEM = pl.BlockSpec(memory_space=pltpu.SMEM)
F32 = jnp.float32
BF16 = jnp.bfloat16
HBM = pl.BlockSpec(memory_space=pltpu.HBM)
PARAMS = pltpu.CompilerParams(vmem_limit_bytes=16 * 1024 * 1024)


def shape(rows, cols, dtype):
    return jax.ShapeDtypeStruct((rows, cols), dtype)


def as_column(row):
    n = row.shape[1]
    return jnp.broadcast_to(row, (n, n)).T


def normalize(raw):
    values = raw.astype(F32)
    scale = lax.rsqrt(jnp.sum(values * values, axis=-1, keepdims=True) + 1e-06)
    return values * scale, scale


def norm_back(unit, scale, upstream):
    return (upstream - unit * jnp.sum(unit * upstream, axis=-1, keepdims=True)) * scale


def matmul_t(a, b):
    return lax.dot_general(a, b, (((1,), (1,)), ((), ())), preferred_element_type=F32)


def matmul(a, b):
    return jnp.dot(a, b, preferred_element_type=F32)


def t_matmul(a, b):
    return lax.dot_general(a, b, (((0,), (0,)), ((), ())), preferred_element_type=F32)


class Scorer:
    def __init__(self, scal_ref, label_ref, place_ref):
        self.temper = jnp.exp(jnp.full((1, 128), scal_ref[0], F32))
        self.bias = scal_ref[1]
        self.labels = label_ref
        self.place = place_ref[0]
        self.columns = {}
        self.sums = None

    def side(self):
        return 1 - 2 * lax.rem(self.place, 2)

    def label_row(self, offset):
        count = self.labels.shape[0]
        at = lax.rem(self.place + offset + count, count)
        return self.labels[pl.ds(at, 1), :]

    def label_column(self, name, offset):
        if name not in self.columns:
            self.columns[name] = as_column(self.label_row(offset).astype(F32))
        return self.columns[name]

    def grads(self, image, text, weight, image_label, text_label, count_it):
        scaled = self.temper * matmul_t(image, text)
        logit = scaled + self.bias
        pos = image_label == text_label.astype(F32)
        small = jnp.exp(-jnp.abs(logit))
        share = 1.0 / (1.0 + small)
        sigmoid = jnp.where(logit >= 0, share, small * share)
        grad = weight * (sigmoid - pos.astype(F32))
        if count_it:
            signed = jnp.where(pos, -logit, logit)
            loss = weight * (jnp.maximum(signed, 0.0) + jnp.log1p(small))
            terms = (loss, grad * scaled, grad)
            self.sums = terms if self.sums is None else tuple(a + b for a, b in zip(self.sums, terms))
        return grad.astype(BF16)

    def store_sums(self, out_ref, more_ref=None):
        out_ref[...] = jnp.zeros_like(out_ref) if more_ref is None else more_ref[...]
        for at in range(3):
            out_ref[at : at + 1, :] += jnp.sum(self.sums[at], axis=0, keepdims=True)


def weight_of(packed, width):
    parts = [packed[:, width + at : width + at + 1].astype(F32) for at in (0, 32, 64)]
    return parts[0] + parts[1] + parts[2]


def text_kernel(text_ref, text_unit_ref):
    text_unit_ref[...] = normalize(text_ref[...])[0].astype(BF16)


def image_kernel(image_ref, weight_ref, text_unit_ref, both_ref):
    width = image_ref.shape[1]
    weight = as_column(weight_ref[...])
    high = weight.astype(BF16)
    rest = weight - high.astype(F32)
    middle = rest.astype(BF16)
    low = (rest - middle.astype(F32)).astype(BF16)
    lane = lax.broadcasted_iota(jnp.int32, weight.shape, 1)
    coded = jnp.where(lane < 32, high.astype(F32), jnp.where(lane < 64, middle.astype(F32), low.astype(F32)))
    both_ref[:, :width] = normalize(image_ref[...])[0].astype(BF16)
    both_ref[:, width : width + 128] = coded.astype(BF16)
    both_ref[:, width + 128 :] = text_unit_ref[...]


def own_kernel(
    scal_ref, place_ref, label_ref, own_ref, cross_ref,
    image_total_ref, text_total_ref, cross_total_ref, sums_ref,
):
    width = cross_ref.shape[1]
    scorer = Scorer(scal_ref, label_ref, place_ref)
    u, v = own_ref[:, :width], own_ref[:, width + 128 :]
    vc = cross_ref[...]
    w = weight_of(own_ref, width)
    row = scorer.label_row(0)
    col = as_column(row.astype(F32))
    g0 = scorer.grads(u, v, w, col, row, True)
    gc = scorer.grads(u, vc, w, col, scorer.label_row(scorer.side()), True)
    image_total_ref[...] = matmul(g0, v) + matmul(gc, vc)
    text_total_ref[...] = t_matmul(g0, u)
    cross_total_ref[...] = t_matmul(gc, u)
    scorer.store_sums(sums_ref)


def early_kernel(
    scal_ref, place_ref, label_ref, own_ref, after_ref, before_ref, cross_ref,
    image_in_ref, text_in_ref, cross_in_ref, sums_in_ref,
    image_total_ref, text_total_ref, cross_total_ref, near_ref, image_far_ref, text_far_ref, sums_ref,
):
    rows, width = cross_ref.shape
    scorer = Scorer(scal_ref, label_ref, place_ref)
    side = scorer.side()
    even = side == 1
    u, v = own_ref[:, :width], own_ref[:, width + 128 :]
    ua, va = after_ref[:, :width], after_ref[:, width + 128 :]
    ub, vb = before_ref[:, :width], before_ref[:, width + 128 :]
    vc = cross_ref[...]
    w, wa, wb = weight_of(own_ref, width), weight_of(after_ref, width), weight_of(before_ref, width)
    row, row_a, row_b = scorer.label_row(0), scorer.label_row(2), scorer.label_row(-2)
    row_c = scorer.label_row(side)
    col, col_a, col_b = as_column(row.astype(F32)), as_column(row_a.astype(F32)), as_column(row_b.astype(F32))
    ux, wx, col_x = jnp.where(even, ub, ua), jnp.where(even, wb, wa), jnp.where(even, col_b, col_a)
    un, wn, col_n = jnp.where(even, ua, ub), jnp.where(even, wa, wb), jnp.where(even, col_a, col_b)
    gx = scorer.grads(ux, vc, wx, col_x, row_c, True)
    gn = scorer.grads(un, vc, wn, col_n, row_c, False)
    cross_total_ref[...] = (cross_in_ref[...] + t_matmul(gx, ux) + t_matmul(gn, un)).astype(BF16)
    ga = scorer.grads(u, va, w, col, row_a, True)
    gb = scorer.grads(u, vb, w, col, row_b, True)
    gfar = scorer.grads(ub, va, wb, col_b, row_a, True)
    ta = scorer.grads(ua, v, wa, col_a, row, False)
    tb = scorer.grads(ub, v, wb, col_b, row, False)
    image_total_ref[...] = image_in_ref[...] + matmul(ga, va) + matmul(gb, vb)
    text_total_ref[...] = text_in_ref[...] + t_matmul(ta, ua) + t_matmul(tb, ub)
    image_far, text_far = matmul(gfar, va), t_matmul(gfar, ub)
    near_ref[:rows, :] = (matmul(gx, vc) + jnp.where(even, image_far, 0.0)).astype(BF16)
    near_ref[rows:, :] = jnp.where(even, 0.0, text_far).astype(BF16)
    image_far_ref[...] = jnp.where(even, 0.0, image_far).astype(BF16)
    text_far_ref[...] = jnp.where(even, text_far, 0.0).astype(BF16)
    scorer.store_sums(sums_ref, sums_in_ref)


def relay_kernel(
    scal_ref, place_ref, label_ref, own_ref, after_ref, before_ref, relay_ref, early_ref,
    image_far_ref, text_far_ref,
    near_g_ref, far_ref, diagonal_ref, sums_ref,
):
    rows, width = relay_ref.shape
    scorer = Scorer(scal_ref, label_ref, place_ref)
    side = scorer.side()
    even = side == 1
    vr = relay_ref[...]
    row_r = scorer.label_row(-side)
    col = as_column(scorer.label_row(0).astype(F32))
    col_x = as_column(scorer.label_row(2 * side).astype(F32))
    ux = jnp.where(even, after_ref[:, :width], before_ref[:, :width])
    wx = jnp.where(even, weight_of(after_ref, width), weight_of(before_ref, width))
    gr = scorer.grads(own_ref[:, :width], vr, weight_of(own_ref, width), col, row_r, True)
    gx = scorer.grads(ux, vr, wx, col_x, row_r, True)
    lane = lax.broadcasted_iota(jnp.int32, (1, 128), 1)
    message = jnp.zeros((1, 128), F32)
    for at in range(3):
        total = jnp.sum(scorer.sums[at], axis=0, keepdims=True) + early_ref[at : at + 1, :]
        message = jnp.where(lane == at, jnp.sum(total, axis=1, keepdims=True), message)
    sums_ref[...] = message
    diagonal_ref[...] = t_matmul(gx, ux).astype(BF16)
    far_ref[:rows, :] = (image_far_ref[...].astype(F32) + matmul(gx, vr)).astype(BF16)
    far_ref[rows:, :] = text_far_ref[...]
    near_g_ref[...] = gr


def middle_kernel(near_any, cross_any, got_ref, sums_ref):
    sums_ref[...] = jnp.sum(got_ref[...], axis=0, keepdims=True)


def final_kernel(
    count, scal_ref, image_ref, text_ref, image_total_ref, text_total_ref, near_g_ref, relay_ref,
    near_ref, cross_ref, far_ref, diagonal_ref, got_ref,
    image_grad_ref, text_grad_ref, stats_ref,
):
    rows, width = image_ref.shape
    temper = jnp.exp(jnp.full((1, 128), scal_ref[0], F32))[:, :1]
    image_total = image_total_ref[...] + matmul(near_g_ref[...], relay_ref[...])
    image_total += near_ref[:rows, :].astype(F32) + far_ref[:rows, :].astype(F32)
    text_total = text_total_ref[...] + (near_ref[rows:, :].astype(F32) + far_ref[rows:, :].astype(F32))
    text_total += cross_ref[...].astype(F32) + diagonal_ref[...].astype(F32)
    for raw_ref, total, out_ref in ((image_ref, image_total, image_grad_ref), (text_ref, text_total, text_grad_ref)):
        unit, scale = normalize(raw_ref[...])
        out_ref[...] = norm_back(unit, scale, temper * total).astype(BF16)
    got = jnp.sum(got_ref[...], axis=0, keepdims=True) / count
    for at in range(3):
        stats_ref[at] = got[0, at]


def call(kernel, ins, outs, name, work, out_specs=None):
    return pl.pallas_call(
        kernel,
        out_shape=outs,
        in_specs=ins,
        out_specs=jax.tree.map(lambda _: VMEM, outs) if out_specs is None else out_specs,
        compiler_params=PARAMS,
        cost_estimate=pl.CostEstimate(flops=work, bytes_accessed=0, transcendentals=0),
        name=name,
    )


def exchanged(row, axis):
    count = lax.axis_size(axis)
    sent = jnp.broadcast_to(row.reshape(1, 1, 128), (count, 1, 128))
    return lax.all_to_all(sent, axis, 0, 0).reshape(count, 128)


def per_device(images, texts, labels, weights, log_temp, bias):
    cycle = lax.axis_size("blk")
    groups = lax.axis_size("group")
    rows, width = images.shape
    place = lax.axis_index("blk").astype(jnp.int32).reshape(1)
    scal = jnp.concatenate([log_temp, bias])
    head = [SMEM, SMEM, VMEM]
    dot = 2 * rows * rows * width

    def passed(value, step_of):
        return lax.ppermute(value, "blk", [(p, (p + step_of(p)) % cycle) for p in range(cycle)])

    def across(value):
        return passed(value, lambda p: 1 - 2 * (p % 2))

    def diagonally(value):
        return passed(value, lambda p: 2 * (p % 2) - 1)

    def far_side(value):
        return passed(value, lambda p: 2 - 4 * (p % 2))

    def near_side(value):
        return passed(value, lambda p: 4 * (p % 2) - 2)

    def upward(value):
        return passed(value, lambda p: 2)

    def downward(value):
        return passed(value, lambda p: -2)

    block, half = shape(rows, width, F32), shape(rows, width, BF16)
    text_unit = call(text_kernel, [VMEM], half, "text", 10 * dot)(texts)
    cross_v = across(text_unit)
    both = call(image_kernel, [VMEM] * 3, shape(rows, 2 * width + 128, BF16), "image", 10 * dot)(
        images, weights.reshape(1, rows), text_unit
    )
    after = downward(both)
    before = upward(both)
    relay_v = far_side(cross_v)
    image_total, text_total, cross_total, sums = call(
        own_kernel, head + [VMEM] * 2, (block,) * 3 + (shape(8, 128, F32),), "own", 200 * dot
    )(scal, place, labels, both, cross_v)
    pair = shape(2 * rows, width, BF16)
    image_total, text_total, cross_total, near, image_far, text_far, sums = call(
        early_kernel,
        head + [VMEM] * 8,
        (block, block, half, pair, half, half, shape(8, 128, F32)),
        "early",
        20 * dot,
    )(scal, place, labels, both, after, before, cross_v, image_total, text_total, cross_total, sums)
    from_cross = across(cross_total)
    from_near = near_side(near)
    near_g, far, diagonal, sums = call(
        relay_kernel, head + [VMEM] * 7, (shape(rows, rows, BF16), pair, half, shape(1, 128, F32)), "relay", 100 * dot
    )(scal, place, labels, both, after, before, relay_v, sums, image_far, text_far)
    from_diagonal = diagonally(diagonal)
    from_far = far_side(far)
    got = exchanged(sums, "group")
    sums = call(middle_kernel, [HBM, HBM, VMEM], shape(1, 128, F32), "middle", 300 * dot)(from_near, from_cross, got)
    got = exchanged(sums, "blk")
    count = float(cycle * groups * rows) * float(rows) * 8.0
    image_grad, text_grad, stats = call(
        functools.partial(final_kernel, count),
        [SMEM] + [VMEM] * 11,
        (half, half, jax.ShapeDtypeStruct((3,), F32)),
        "final",
        10 * dot,
        (VMEM, VMEM, SMEM),
    )(
        scal, images, texts, image_total, text_total, near_g, relay_v,
        from_near, from_cross, from_far, from_diagonal, got,
    )
    return image_grad, text_grad, stats


def solution(mesh):
    rows = P(("blk", "group"), None)
    in_specs = (rows, rows, P(None, "group"), P(("blk", "group")), P(), P())
    return jax.shard_map(per_device, mesh=mesh, in_specs=in_specs, out_specs=(rows, rows, P()), check_vma=False)
```

```python
import functools

import jax
import jax.numpy as jnp
from jax import lax
from jax.experimental import pallas as pl
from jax.experimental.pallas import tpu as pltpu
from jax.sharding import PartitionSpec as P

VMEM = pl.BlockSpec(memory_space=pltpu.VMEM)
SMEM = pl.BlockSpec(memory_space=pltpu.SMEM)
F32 = jnp.float32
BF16 = jnp.bfloat16
HBM = pl.BlockSpec(memory_space=pltpu.HBM)
PARAMS = pltpu.CompilerParams(vmem_limit_bytes=16 * 1024 * 1024)


def shape(rows, cols, dtype):
    return jax.ShapeDtypeStruct((rows, cols), dtype)


def as_column(row):
    n = row.shape[1]
    return jnp.broadcast_to(row, (n, n)).T


def normalize(raw):
    values = raw.astype(F32)
    scale = lax.rsqrt(jnp.sum(values * values, axis=-1, keepdims=True) + 1e-06)
    return values * scale, scale


def norm_back(unit, scale, upstream):
    return (upstream - unit * jnp.sum(unit * upstream, axis=-1, keepdims=True)) * scale


def matmul_t(a, b):
    return lax.dot_general(a, b, (((1,), (1,)), ((), ())), preferred_element_type=F32)


def matmul(a, b):
    return jnp.dot(a, b, preferred_element_type=F32)


def t_matmul(a, b):
    return lax.dot_general(a, b, (((0,), (0,)), ((), ())), preferred_element_type=F32)


class Scorer:
    def __init__(self, scal_ref, label_ref, place_ref):
        self.temper = jnp.exp(jnp.full((1, 128), scal_ref[0], F32))
        self.bias = scal_ref[1]
        self.labels = label_ref
        self.place = place_ref[0]
        self.columns = {}
        self.sums = None

    def side(self):
        return 1 - 2 * lax.rem(self.place, 2)

    def label_row(self, offset):
        count = self.labels.shape[0]
        at = lax.rem(self.place + offset + count, count)
        return self.labels[pl.ds(at, 1), :]

    def label_column(self, name, offset):
        if name not in self.columns:
            self.columns[name] = as_column(self.label_row(offset).astype(F32))
        return self.columns[name]

    def grads(self, image, text, weight, image_label, text_label, count_it):
        scaled = self.temper * matmul_t(image, text)
        logit = scaled + self.bias
        pos = image_label == text_label.astype(F32)
        small = jnp.exp(-jnp.abs(logit))
        share = 1.0 / (1.0 + small)
        sigmoid = jnp.where(logit >= 0, share, small * share)
        grad = weight * (sigmoid - pos.astype(F32))
        if count_it:
            signed = jnp.where(pos, -logit, logit)
            loss = weight * (jnp.maximum(signed, 0.0) + jnp.log1p(small))
            terms = (loss, grad * scaled, grad)
            self.sums = terms if self.sums is None else tuple(a + b for a, b in zip(self.sums, terms))
        return grad.astype(BF16)

    def store_sums(self, out_ref, more_ref=None):
        out_ref[...] = jnp.zeros_like(out_ref) if more_ref is None else more_ref[...]
        for at in range(3):
            out_ref[at : at + 1, :] += jnp.sum(self.sums[at], axis=0, keepdims=True)


def weight_of(packed, width):
    parts = [packed[:, width + at : width + at + 1].astype(F32) for at in (0, 32, 64)]
    return parts[0] + parts[1] + parts[2]


def text_kernel(text_ref, text_unit_ref):
    text_unit_ref[...] = normalize(text_ref[...])[0].astype(BF16)


def image_kernel(image_ref, weight_ref, text_unit_ref, image_pack_ref, both_ref):
    width = image_ref.shape[1]
    u = normalize(image_ref[...])[0].astype(BF16)
    weight = as_column(weight_ref[...])
    high = weight.astype(BF16)
    rest = weight - high.astype(F32)
    middle = rest.astype(BF16)
    low = (rest - middle.astype(F32)).astype(BF16)
    lane = lax.broadcasted_iota(jnp.int32, weight.shape, 1)
    coded = jnp.where(lane < 32, high.astype(F32), jnp.where(lane < 64, middle.astype(F32), low.astype(F32))).astype(BF16)
    image_pack_ref[:, :width] = u
    image_pack_ref[:, width:] = coded
    both_ref[:, :width] = u
    both_ref[:, width : width + 128] = coded
    both_ref[:, width + 128 :] = text_unit_ref[...]


def own_kernel(scal_ref, place_ref, label_ref, own_ref, cross_ref, image_total_ref, text_total_ref, sums_ref):
    width = cross_ref.shape[1]
    scorer = Scorer(scal_ref, label_ref, place_ref)
    u, v = own_ref[:, :width], own_ref[:, width + 128 :]
    vc = cross_ref[...]
    w = weight_of(own_ref, width)
    row = scorer.label_row(0)
    col = as_column(row.astype(F32))
    g0 = scorer.grads(u, v, w, col, row, True)
    gc = scorer.grads(u, vc, w, col, scorer.label_row(scorer.side()), True)
    image_total_ref[...] = matmul(g0, v) + matmul(gc, vc)
    text_total_ref[...] = t_matmul(g0, u)
    scorer.store_sums(sums_ref)


def early_kernel(
    scal_ref, place_ref, label_ref, own_ref, after_ref, before_ref, cross_ref,
    image_in_ref, text_in_ref, sums_in_ref,
    image_total_ref, text_total_ref, cross_g_ref, four_g_ref, sums_ref,
):
    rows, width = cross_ref.shape
    scorer = Scorer(scal_ref, label_ref, place_ref)
    side = scorer.side()
    even = side == 1
    u, v = own_ref[:, :width], own_ref[:, width + 128 :]
    ua, va = after_ref[:, :width], after_ref[:, width + 128 :]
    ub, vb = before_ref[:, :width], before_ref[:, width + 128 :]
    vc = cross_ref[...]
    w, wa, wb = weight_of(own_ref, width), weight_of(after_ref, width), weight_of(before_ref, width)
    row, row_a, row_b = scorer.label_row(0), scorer.label_row(2), scorer.label_row(-2)
    row_c = scorer.label_row(side)
    col, col_a, col_b = as_column(row.astype(F32)), as_column(row_a.astype(F32)), as_column(row_b.astype(F32))
    ga = scorer.grads(u, va, w, col, row_a, True)
    gb = scorer.grads(u, vb, w, col, row_b, True)
    gfar = scorer.grads(ub, va, wb, col_b, row_a, True)
    ux = jnp.where(even, ub, ua)
    gx = scorer.grads(ux, vc, jnp.where(even, wb, wa), jnp.where(even, col_b, col_a), row_c, True)
    ta = scorer.grads(ua, v, wa, col_a, row, False)
    tb = scorer.grads(ub, v, wb, col_b, row, False)
    image_total_ref[...] = image_in_ref[...] + matmul(ga, va) + matmul(gb, vb)
    text_total_ref[...] = text_in_ref[...] + t_matmul(ta, ua) + t_matmul(tb, ub)
    cross_g_ref[...], four_g_ref[...] = gx, gfar
    scorer.store_sums(sums_ref, sums_in_ref)


def relay_kernel(
    scal_ref, place_ref, label_ref, own_ref, after_ref, before_ref, relay_ref, early_ref,
    near_ref, far_ref, sums_ref,
):
    width = relay_ref.shape[1]
    scorer = Scorer(scal_ref, label_ref, place_ref)
    side = scorer.side()
    even = side == 1
    vr = relay_ref[...]
    row_r = scorer.label_row(-side)
    col = as_column(scorer.label_row(0).astype(F32))
    col_x = as_column(scorer.label_row(2 * side).astype(F32))
    near_ref[...] = scorer.grads(own_ref[:, :width], vr, weight_of(own_ref, width), col, row_r, True)
    ux = jnp.where(even, after_ref[:, :width], before_ref[:, :width])
    wx = jnp.where(even, weight_of(after_ref, width), weight_of(before_ref, width))
    far_ref[...] = scorer.grads(ux, vr, wx, col_x, row_r, True)
    lane = lax.broadcasted_iota(jnp.int32, (1, 128), 1)
    message = jnp.zeros((1, 128), F32)
    for at in range(3):
        total = jnp.sum(scorer.sums[at], axis=0, keepdims=True) + early_ref[at : at + 1, :]
        message = jnp.where(lane == at, jnp.sum(total, axis=1, keepdims=True), message)
    sums_ref[...] = jnp.broadcast_to(message.reshape(1, 1, 128), sums_ref.shape)


def late_kernel(
    scal_ref, place_ref, label_any, own_any, after_any, before_any, cross_any, relay_any, relay_v_any,
    far_g_any, cross_v_any, far_cross_any, four_any,
    to_up_ref, to_down_ref, cross_g_ref, relay_g_ref,
    label_ref, v_ref, va_ref, before_ref, cross_ref, relay_ref, relay_v_ref, far_g_ref, cross_v_ref, far_cross_ref, four_ref,
    sems,
):
    rows, width = relay_v_ref.shape
    text_part = (slice(None), pl.ds(width + 128, width))
    copies = [
        pltpu.make_async_copy(source, target, sems.at[at])
        for at, (source, target) in enumerate((
            (label_any, label_ref),
            (cross_any, cross_ref),
            (before_any, before_ref),
            (after_any.at[text_part], va_ref),
            (own_any.at[text_part], v_ref),
            (relay_any, relay_ref),
            (far_g_any, far_g_ref),
            (relay_v_any, relay_v_ref),
            (cross_v_any, cross_v_ref),
            (far_cross_any, far_cross_ref),
            (four_any, four_ref),
        ))
    ]
    for copy in copies:
        copy.start()
    for copy in copies[:5]:
        copy.wait()
    scorer = Scorer(scal_ref, label_ref, place_ref)
    side = scorer.side()
    even = side == 1
    v, va, vb = v_ref[...], va_ref[...], before_ref[:, width + 128 :]
    uc = cross_ref[:, :width]
    wc = weight_of(cross_ref, width)
    col_c = as_column(scorer.label_row(side).astype(F32))
    col_r = as_column(scorer.label_row(-side).astype(F32))
    row, row_a, row_b = scorer.label_row(0), scorer.label_row(2), scorer.label_row(-2)
    gcx = scorer.grads(uc, jnp.where(even, vb, va), wc, col_c, jnp.where(even, row_b, row_a), False)
    gc = scorer.grads(uc, v, wc, col_c, row, False)
    for copy in copies[5:]:
        copy.wait()
    ur, wr = relay_ref[:, :width], weight_of(relay_ref, width)
    grx = scorer.grads(ur, jnp.where(even, va, vb), wr, col_r, jnp.where(even, row_a, row_b), False)
    gr = scorer.grads(ur, v, wr, col_r, row, False)
    far_text_c, far_text_r = t_matmul(gcx, uc), t_matmul(grx, ur)
    far_image_r = matmul(far_g_ref[...], relay_v_ref[...])
    far_image_c = matmul(far_cross_ref[...], cross_v_ref[...])
    g = four_ref[...]
    to_up_ref[:rows, :] = jnp.where(even, far_image_r, far_image_c).astype(BF16)
    to_up_ref[rows:, :] = (t_matmul(g, before_ref[:, :width]) + jnp.where(even, far_text_r, far_text_c)).astype(BF16)
    to_down_ref[:rows, :] = (matmul(g, va) + jnp.where(even, far_image_c, far_image_r)).astype(BF16)
    to_down_ref[rows:, :] = jnp.where(even, far_text_c, far_text_r).astype(BF16)
    cross_g_ref[...], relay_g_ref[...] = gc, gr


def middle_kernel(got_ref, sums_ref):
    total = jnp.sum(got_ref[...], axis=0, keepdims=True)
    sums_ref[...] = jnp.broadcast_to(total.reshape(1, 1, 128), sums_ref.shape)


def final_kernel(
    count, scal_ref, image_ref, text_ref, image_total_ref, text_total_ref, near_g_ref, relay_v_ref,
    cross_g_ref, cross_ref, relay_g_ref, relay_ref, up_ref, down_ref, got_ref,
    image_grad_ref, text_grad_ref, stats_ref,
):
    rows, width = image_ref.shape
    temper = jnp.exp(jnp.full((1, 128), scal_ref[0], F32))[:, :1]
    image_more = matmul(near_g_ref[...], relay_v_ref[...])
    text_more = t_matmul(cross_g_ref[...], cross_ref[:, :width]) + t_matmul(relay_g_ref[...], relay_ref[:, :width])
    for raw_ref, total_ref, more, out_ref, at in (
        (image_ref, image_total_ref, image_more, image_grad_ref, 0),
        (text_ref, text_total_ref, text_more, text_grad_ref, rows),
    ):
        total = total_ref[...] + more + up_ref[at : at + rows, :].astype(F32) + down_ref[at : at + rows, :].astype(F32)
        unit, scale = normalize(raw_ref[...])
        out_ref[...] = norm_back(unit, scale, temper * total).astype(BF16)
    got = jnp.sum(got_ref[...], axis=0, keepdims=True) / count
    for at in range(3):
        stats_ref[at] = got[0, at]


def call(kernel, ins, outs, name, work, out_specs=None, scratch=()):
    return pl.pallas_call(
        kernel,
        out_shape=outs,
        in_specs=ins,
        out_specs=jax.tree.map(lambda _: VMEM, outs) if out_specs is None else out_specs,
        scratch_shapes=scratch,
        compiler_params=PARAMS,
        cost_estimate=pl.CostEstimate(flops=work, bytes_accessed=0, transcendentals=0),
        name=name,
    )


def exchanged(sent, axis):
    return lax.all_to_all(sent, axis, 0, 0).reshape(sent.shape[0], 128)


def per_device(images, texts, labels, weights, log_temp, bias):
    cycle = lax.axis_size("blk")
    groups = lax.axis_size("group")
    rows, width = images.shape
    place = lax.axis_index("blk").astype(jnp.int32).reshape(1)
    scal = jnp.concatenate([log_temp, bias])
    head = [SMEM, SMEM, VMEM]
    dot = 2 * rows * rows * width

    def passed(value, step_of):
        return lax.ppermute(value, "blk", [(p, (p + step_of(p)) % cycle) for p in range(cycle)])

    def across(value):
        return passed(value, lambda p: 1 - 2 * (p % 2))

    def relayed(value):
        return passed(value, lambda p: 2 - 4 * (p % 2))

    def upward(value):
        return passed(value, lambda p: 2)

    def downward(value):
        return passed(value, lambda p: -2)

    block, square = shape(rows, width, F32), shape(rows, rows, BF16)
    text_unit = call(text_kernel, [VMEM], shape(rows, width, BF16), "text", 10 * dot)(texts)
    cross_v = across(text_unit)
    image_pack, both = call(
        image_kernel,
        [VMEM] * 3,
        (shape(rows, width + 128, BF16), shape(rows, 2 * width + 128, BF16)),
        "image",
        10 * dot,
    )(images, weights.reshape(1, rows), text_unit)
    after = downward(both)
    before = upward(both)
    cross_u = across(image_pack)
    relay_v = relayed(cross_v)
    image_total, text_total, sums = call(
        own_kernel, head + [VMEM] * 2, (block,) * 2 + (shape(8, 128, F32),), "own", 150 * dot
    )(scal, place, labels, both, cross_v)
    image_total, text_total, far_cross_g, four_g, sums = call(
        early_kernel, head + [VMEM] * 7, (block, block, square, square, shape(8, 128, F32)), "early", 20 * dot
    )(scal, place, labels, both, after, before, cross_v, image_total, text_total, sums)
    near_g, far_g, sums = call(
        relay_kernel,
        head + [VMEM] * 5,
        (square, square, jax.ShapeDtypeStruct((groups, 1, 128), F32)),
        "relay", 10 * dot
    )(scal, place, labels, both, after, before, relay_v, sums)
    cross_u, sums = lax.optimization_barrier((cross_u, sums))
    relay_u = relayed(cross_u)
    got = exchanged(sums, "group")
    half, pack = pltpu.VMEM((rows, width), BF16), pltpu.VMEM((rows, width + 128), BF16)
    scratch = [pltpu.VMEM(labels.shape, jnp.int32), half, half, pltpu.VMEM(both.shape, BF16), pack, pack, half]
    block_g = pltpu.VMEM((rows, rows), BF16)
    scratch += [block_g, half, block_g, block_g]
    to_up, to_down, cross_g, relay_g = call(
        late_kernel,
        [SMEM, SMEM] + [HBM] * 11,
        (shape(2 * rows, width, BF16),) * 2 + (shape(rows, rows, BF16),) * 2,
        "late",
        400 * dot,
        scratch=scratch + [pltpu.SemaphoreType.DMA((11,))],
    )(scal, place, labels, both, after, before, cross_u, relay_u, relay_v, far_g, cross_v, far_cross_g, four_g)
    from_below = upward(to_up)
    from_above = downward(to_down)
    sums = call(middle_kernel, [VMEM], jax.ShapeDtypeStruct((cycle, 1, 128), F32), "middle", 300 * dot)(got)
    got = exchanged(sums, "blk")
    count = float(cycle * groups * rows) * float(rows) * 8.0
    image_grad, text_grad, stats = call(
        functools.partial(final_kernel, count),
        [SMEM] + [VMEM] * 13,
        (shape(rows, width, BF16),) * 2 + (jax.ShapeDtypeStruct((3,), F32),),
        "final",
        10 * dot,
        (VMEM, VMEM, SMEM),
    )(
        scal, images, texts, image_total, text_total, near_g, relay_v, cross_g, cross_u, relay_g, relay_u,
        from_below, from_above, got,
    )
    return image_grad, text_grad, stats


def solution(mesh):
    rows = P(("blk", "group"), None)
    in_specs = (rows, rows, P(None, "group"), P(("blk", "group")), P(), P())
    return jax.shard_map(per_device, mesh=mesh, in_specs=in_specs, out_specs=(rows, rows, P()), check_vma=False)
```

```python
import functools

import jax
import jax.numpy as jnp
from jax import lax
from jax.experimental import pallas as pl
from jax.experimental.pallas import tpu as pltpu
from jax.sharding import PartitionSpec as P

VMEM = pl.BlockSpec(memory_space=pltpu.VMEM)
SMEM = pl.BlockSpec(memory_space=pltpu.SMEM)
F32 = jnp.float32
BF16 = jnp.bfloat16
HBM = pl.BlockSpec(memory_space=pltpu.HBM)
PARAMS = pltpu.CompilerParams(vmem_limit_bytes=16 * 1024 * 1024)


def shape(rows, cols, dtype):
    return jax.ShapeDtypeStruct((rows, cols), dtype)


def as_column(row):
    n = row.shape[1]
    return jnp.broadcast_to(row, (n, n)).T


def normalize(raw):
    values = raw.astype(F32)
    scale = lax.rsqrt(jnp.sum(values * values, axis=-1, keepdims=True) + 1e-06)
    return values * scale, scale


def norm_back(unit, scale, upstream):
    return (upstream - unit * jnp.sum(unit * upstream, axis=-1, keepdims=True)) * scale


def matmul_t(a, b):
    return lax.dot_general(a, b, (((1,), (1,)), ((), ())), preferred_element_type=F32)


def matmul(a, b):
    return jnp.dot(a, b, preferred_element_type=F32)


def t_matmul(a, b):
    return lax.dot_general(a, b, (((0,), (0,)), ((), ())), preferred_element_type=F32)


class Scorer:
    def __init__(self, scal_ref, label_ref, place_ref):
        self.temper = jnp.exp(jnp.full((1, 128), scal_ref[0], F32))
        self.bias = scal_ref[1]
        self.labels = label_ref
        self.place = place_ref[0]
        self.columns = {}
        self.sums = None

    def side(self):
        return 1 - 2 * lax.rem(self.place, 2)

    def label_row(self, offset):
        count = self.labels.shape[0]
        at = lax.rem(self.place + offset + count, count)
        return self.labels[pl.ds(at, 1), :]

    def label_column(self, name, offset):
        if name not in self.columns:
            self.columns[name] = as_column(self.label_row(offset).astype(F32))
        return self.columns[name]

    def grads(self, image, text, weight, image_label, text_label, count_it):
        scaled = self.temper * matmul_t(image, text)
        logit = scaled + self.bias
        pos = image_label == text_label.astype(F32)
        small = jnp.exp(-jnp.abs(logit))
        share = 1.0 / (1.0 + small)
        sigmoid = jnp.where(logit >= 0, share, small * share)
        grad = weight * (sigmoid - pos.astype(F32))
        if count_it:
            signed = jnp.where(pos, -logit, logit)
            loss = weight * (jnp.maximum(signed, 0.0) + jnp.log1p(small))
            terms = (loss, grad * scaled, grad)
            self.sums = terms if self.sums is None else tuple(a + b for a, b in zip(self.sums, terms))
        return grad.astype(BF16)

    def store_sums(self, out_ref, more_ref=None):
        out_ref[...] = jnp.zeros_like(out_ref) if more_ref is None else more_ref[...]
        for at in range(3):
            out_ref[at : at + 1, :] += jnp.sum(self.sums[at], axis=0, keepdims=True)


def weight_of(packed, width):
    parts = [packed[:, width + at : width + at + 1].astype(F32) for at in (0, 32, 64)]
    return parts[0] + parts[1] + parts[2]


def text_kernel(text_ref, text_unit_ref):
    text_unit_ref[...] = normalize(text_ref[...])[0].astype(BF16)


def image_kernel(image_ref, weight_ref, text_unit_ref, image_pack_ref, both_ref):
    width = image_ref.shape[1]
    u = normalize(image_ref[...])[0].astype(BF16)
    weight = as_column(weight_ref[...])
    high = weight.astype(BF16)
    rest = weight - high.astype(F32)
    middle = rest.astype(BF16)
    low = (rest - middle.astype(F32)).astype(BF16)
    lane = lax.broadcasted_iota(jnp.int32, weight.shape, 1)
    coded = jnp.where(lane < 32, high.astype(F32), jnp.where(lane < 64, middle.astype(F32), low.astype(F32))).astype(BF16)
    image_pack_ref[:, :width] = u
    image_pack_ref[:, width:] = coded
    both_ref[:, :width] = u
    both_ref[:, width : width + 128] = coded
    both_ref[:, width + 128 :] = text_unit_ref[...]


def own_kernel(scal_ref, place_ref, label_ref, own_ref, cross_ref, image_total_ref, text_total_ref, sums_ref):
    width = cross_ref.shape[1]
    scorer = Scorer(scal_ref, label_ref, place_ref)
    u, v = own_ref[:, :width], own_ref[:, width + 128 :]
    vc = cross_ref[...]
    w = weight_of(own_ref, width)
    row = scorer.label_row(0)
    col = as_column(row.astype(F32))
    g0 = scorer.grads(u, v, w, col, row, True)
    gc = scorer.grads(u, vc, w, col, scorer.label_row(scorer.side()), True)
    image_total_ref[...] = matmul(g0, v) + matmul(gc, vc)
    text_total_ref[...] = t_matmul(g0, u)
    scorer.store_sums(sums_ref)


def early_kernel(
    scal_ref, place_ref, label_ref, own_ref, before_ref, after_ref, cross_ref,
    image_in_ref, text_in_ref, sums_in_ref,
    image_total_ref, text_total_ref, cross_g_ref, four_g_ref, sums_ref,
):
    rows, width = cross_ref.shape
    scorer = Scorer(scal_ref, label_ref, place_ref)
    side = scorer.side()
    even = side == 1
    u, v = own_ref[:, :width], own_ref[:, width + 128 :]
    ua, va = after_ref[:, :width], after_ref[:, width + 128 :]
    ub, vb = before_ref[:, :width], before_ref[:, width + 128 :]
    vc = cross_ref[...]
    w, wa, wb = weight_of(own_ref, width), weight_of(after_ref, width), weight_of(before_ref, width)
    row, row_a, row_b = scorer.label_row(0), scorer.label_row(2), scorer.label_row(-2)
    row_c = scorer.label_row(side)
    col, col_a, col_b = as_column(row.astype(F32)), as_column(row_a.astype(F32)), as_column(row_b.astype(F32))
    ga = scorer.grads(u, va, w, col, row_a, True)
    gb = scorer.grads(u, vb, w, col, row_b, True)
    gfar = scorer.grads(ub, va, wb, col_b, row_a, True)
    ux = jnp.where(even, ub, ua)
    gx = scorer.grads(ux, vc, jnp.where(even, wb, wa), jnp.where(even, col_b, col_a), row_c, True)
    ta = scorer.grads(ua, v, wa, col_a, row, False)
    tb = scorer.grads(ub, v, wb, col_b, row, False)
    image_total_ref[...] = image_in_ref[...] + matmul(ga, va) + matmul(gb, vb)
    text_total_ref[...] = text_in_ref[...] + t_matmul(ta, ua) + t_matmul(tb, ub)
    cross_g_ref[...], four_g_ref[...] = gx, gfar
    scorer.store_sums(sums_ref, sums_in_ref)


def relay_kernel(
    scal_ref, place_ref, label_ref, own_ref, after_ref, before_ref, relay_ref, early_ref,
    near_ref, far_ref, sums_ref,
):
    width = relay_ref.shape[1]
    scorer = Scorer(scal_ref, label_ref, place_ref)
    side = scorer.side()
    even = side == 1
    vr = relay_ref[...]
    row_r = scorer.label_row(-side)
    col = as_column(scorer.label_row(0).astype(F32))
    col_x = as_column(scorer.label_row(2 * side).astype(F32))
    near_ref[...] = scorer.grads(own_ref[:, :width], vr, weight_of(own_ref, width), col, row_r, True)
    ux = jnp.where(even, after_ref[:, :width], before_ref[:, :width])
    wx = jnp.where(even, weight_of(after_ref, width), weight_of(before_ref, width))
    far_ref[...] = scorer.grads(ux, vr, wx, col_x, row_r, True)
    lane = lax.broadcasted_iota(jnp.int32, (1, 128), 1)
    message = jnp.zeros((1, 128), F32)
    for at in range(3):
        total = jnp.sum(scorer.sums[at], axis=0, keepdims=True) + early_ref[at : at + 1, :]
        message = jnp.where(lane == at, jnp.sum(total, axis=1, keepdims=True), message)
    sums_ref[...] = jnp.broadcast_to(message.reshape(1, 1, 128), sums_ref.shape)


def late_kernel(
    scal_ref, place_ref, label_any, own_any, after_any, before_any, cross_any, relay_any, relay_v_any,
    far_g_any, cross_v_any, far_cross_any, four_any,
    to_up_ref, to_down_ref, cross_g_ref, relay_g_ref,
    label_ref, v_ref, va_ref, before_ref, cross_ref, relay_ref, relay_v_ref, far_g_ref, cross_v_ref, far_cross_ref, four_ref,
    sems,
):
    rows, width = relay_v_ref.shape
    text_part = (slice(None), pl.ds(width + 128, width))
    copies = [
        pltpu.make_async_copy(source, target, sems.at[at])
        for at, (source, target) in enumerate((
            (label_any, label_ref),
            (cross_any, cross_ref),
            (before_any, before_ref),
            (after_any.at[text_part], va_ref),
            (own_any.at[text_part], v_ref),
            (relay_any, relay_ref),
            (far_g_any, far_g_ref),
            (relay_v_any, relay_v_ref),
            (cross_v_any, cross_v_ref),
            (far_cross_any, far_cross_ref),
            (four_any, four_ref),
        ))
    ]
    for copy in copies:
        copy.start()
    for copy in copies[:5]:
        copy.wait()
    scorer = Scorer(scal_ref, label_ref, place_ref)
    side = scorer.side()
    even = side == 1
    v, va, vb = v_ref[...], va_ref[...], before_ref[:, width + 128 :]
    uc = cross_ref[:, :width]
    wc = weight_of(cross_ref, width)
    col_c = as_column(scorer.label_row(side).astype(F32))
    col_r = as_column(scorer.label_row(-side).astype(F32))
    row, row_a, row_b = scorer.label_row(0), scorer.label_row(2), scorer.label_row(-2)
    gcx = scorer.grads(uc, jnp.where(even, vb, va), wc, col_c, jnp.where(even, row_b, row_a), False)
    gc = scorer.grads(uc, v, wc, col_c, row, False)
    for copy in copies[5:]:
        copy.wait()
    ur, wr = relay_ref[:, :width], weight_of(relay_ref, width)
    grx = scorer.grads(ur, jnp.where(even, va, vb), wr, col_r, jnp.where(even, row_a, row_b), False)
    gr = scorer.grads(ur, v, wr, col_r, row, False)
    far_text_c, far_text_r = t_matmul(gcx, uc), t_matmul(grx, ur)
    far_image_r = matmul(far_g_ref[...], relay_v_ref[...])
    far_image_c = matmul(far_cross_ref[...], cross_v_ref[...])
    g = four_ref[...]
    to_up_ref[:rows, :] = jnp.where(even, far_image_r, far_image_c).astype(BF16)
    to_up_ref[rows:, :] = (t_matmul(g, before_ref[:, :width]) + jnp.where(even, far_text_r, far_text_c)).astype(BF16)
    to_down_ref[:rows, :] = (matmul(g, va) + jnp.where(even, far_image_c, far_image_r)).astype(BF16)
    to_down_ref[rows:, :] = jnp.where(even, far_text_c, far_text_r).astype(BF16)
    cross_g_ref[...], relay_g_ref[...] = gc, gr


def middle_kernel(got_ref, sums_ref):
    total = jnp.sum(got_ref[...], axis=0, keepdims=True)
    sums_ref[...] = jnp.broadcast_to(total.reshape(1, 1, 128), sums_ref.shape)


def final_kernel(
    count, scal_ref, image_ref, text_ref, image_total_ref, text_total_ref, near_g_ref, relay_v_ref,
    cross_g_ref, cross_ref, relay_g_ref, relay_ref, up_ref, down_ref, got_ref,
    image_grad_ref, text_grad_ref, stats_ref,
):
    rows, width = image_ref.shape
    temper = jnp.exp(jnp.full((1, 128), scal_ref[0], F32))[:, :1]
    image_more = matmul(near_g_ref[...], relay_v_ref[...])
    text_more = t_matmul(cross_g_ref[...], cross_ref[:, :width]) + t_matmul(relay_g_ref[...], relay_ref[:, :width])
    for raw_ref, total_ref, more, out_ref, at in (
        (image_ref, image_total_ref, image_more, image_grad_ref, 0),
        (text_ref, text_total_ref, text_more, text_grad_ref, rows),
    ):
        total = total_ref[...] + more + up_ref[at : at + rows, :].astype(F32) + down_ref[at : at + rows, :].astype(F32)
        unit, scale = normalize(raw_ref[...])
        out_ref[...] = norm_back(unit, scale, temper * total).astype(BF16)
    got = jnp.sum(got_ref[...], axis=0, keepdims=True) / count
    for at in range(3):
        stats_ref[at] = got[0, at]


def call(kernel, ins, outs, name, work, out_specs=None, scratch=()):
    return pl.pallas_call(
        kernel,
        out_shape=outs,
        in_specs=ins,
        out_specs=jax.tree.map(lambda _: VMEM, outs) if out_specs is None else out_specs,
        scratch_shapes=scratch,
        compiler_params=PARAMS,
        cost_estimate=pl.CostEstimate(flops=work, bytes_accessed=0, transcendentals=0),
        name=name,
    )


def exchanged(sent, axis):
    return lax.all_to_all(sent, axis, 0, 0).reshape(sent.shape[0], 128)


def per_device(images, texts, labels, weights, log_temp, bias):
    cycle = lax.axis_size("blk")
    groups = lax.axis_size("group")
    rows, width = images.shape
    place = lax.axis_index("blk").astype(jnp.int32).reshape(1)
    scal = jnp.concatenate([log_temp, bias])
    head = [SMEM, SMEM, VMEM]
    dot = 2 * rows * rows * width

    def passed(value, step_of):
        return lax.ppermute(value, "blk", [(p, (p + step_of(p)) % cycle) for p in range(cycle)])

    def across(value):
        return passed(value, lambda p: 1 - 2 * (p % 2))

    def relayed(value):
        return passed(value, lambda p: 2 - 4 * (p % 2))

    def upward(value):
        return passed(value, lambda p: 2)

    def downward(value):
        return passed(value, lambda p: -2)

    block, square = shape(rows, width, F32), shape(rows, rows, BF16)
    text_unit = call(text_kernel, [VMEM], shape(rows, width, BF16), "text", 10 * dot)(texts)
    cross_v = across(text_unit)
    image_pack, both = call(
        image_kernel,
        [VMEM] * 3,
        (shape(rows, width + 128, BF16), shape(rows, 2 * width + 128, BF16)),
        "image",
        10 * dot,
    )(images, weights.reshape(1, rows), text_unit)
    after = downward(both)
    before = upward(both)
    cross_u = across(image_pack)
    relay_v = relayed(cross_v)
    image_total, text_total, sums = call(
        own_kernel, head + [VMEM] * 2, (block,) * 2 + (shape(8, 128, F32),), "own", 150 * dot
    )(scal, place, labels, both, cross_v)
    image_total, text_total, far_cross_g, four_g, sums = call(
        early_kernel, head + [VMEM] * 7, (block, block, square, square, shape(8, 128, F32)), "early", 20 * dot
    )(scal, place, labels, both, before, after, cross_v, image_total, text_total, sums)
    near_g, far_g, sums = call(
        relay_kernel,
        head + [VMEM] * 5,
        (square, square, jax.ShapeDtypeStruct((groups, 1, 128), F32)),
        "relay", 10 * dot
    )(scal, place, labels, both, after, before, relay_v, sums)
    cross_u, sums = lax.optimization_barrier((cross_u, sums))
    relay_u = relayed(cross_u)
    got = exchanged(sums, "group")
    half, pack = pltpu.VMEM((rows, width), BF16), pltpu.VMEM((rows, width + 128), BF16)
    scratch = [pltpu.VMEM(labels.shape, jnp.int32), half, half, pltpu.VMEM(both.shape, BF16), pack, pack, half]
    block_g = pltpu.VMEM((rows, rows), BF16)
    scratch += [block_g, half, block_g, block_g]
    to_up, to_down, cross_g, relay_g = call(
        late_kernel,
        [SMEM, SMEM] + [HBM] * 11,
        (shape(2 * rows, width, BF16),) * 2 + (shape(rows, rows, BF16),) * 2,
        "late",
        400 * dot,
        scratch=scratch + [pltpu.SemaphoreType.DMA((11,))],
    )(scal, place, labels, both, after, before, cross_u, relay_u, relay_v, far_g, cross_v, far_cross_g, four_g)
    from_below = upward(to_up)
    from_above = downward(to_down)
    sums = call(middle_kernel, [VMEM], jax.ShapeDtypeStruct((cycle, 1, 128), F32), "middle", 300 * dot)(got)
    got = exchanged(sums, "blk")
    count = float(cycle * groups * rows) * float(rows) * 8.0
    image_grad, text_grad, stats = call(
        functools.partial(final_kernel, count),
        [SMEM] + [VMEM] * 13,
        (shape(rows, width, BF16),) * 2 + (jax.ShapeDtypeStruct((3,), F32),),
        "final",
        10 * dot,
        (VMEM, VMEM, SMEM),
    )(
        scal, images, texts, image_total, text_total, near_g, relay_v, cross_g, cross_u, relay_g, relay_u,
        from_below, from_above, got,
    )
    return image_grad, text_grad, stats


def solution(mesh):
    rows = P(("blk", "group"), None)
    in_specs = (rows, rows, P(None, "group"), P(("blk", "group")), P(), P())
    return jax.shard_map(per_device, mesh=mesh, in_specs=in_specs, out_specs=(rows, rows, P()), check_vma=False)
```

```python
import functools

import jax
import jax.numpy as jnp
from jax import lax
from jax.experimental import pallas as pl
from jax.experimental.pallas import tpu as pltpu
from jax.sharding import PartitionSpec as P

VMEM = pl.BlockSpec(memory_space=pltpu.VMEM)
SMEM = pl.BlockSpec(memory_space=pltpu.SMEM)
F32 = jnp.float32
BF16 = jnp.bfloat16
HBM = pl.BlockSpec(memory_space=pltpu.HBM)
PARAMS = pltpu.CompilerParams(vmem_limit_bytes=16 * 1024 * 1024)


def shape(rows, cols, dtype):
    return jax.ShapeDtypeStruct((rows, cols), dtype)


def as_column(row):
    n = row.shape[1]
    return jnp.broadcast_to(row, (n, n)).T


def normalize(raw):
    values = raw.astype(F32)
    scale = lax.rsqrt(jnp.sum(values * values, axis=-1, keepdims=True) + 1e-06)
    return values * scale, scale


def norm_back(unit, scale, upstream):
    return (upstream - unit * jnp.sum(unit * upstream, axis=-1, keepdims=True)) * scale


def matmul_t(a, b):
    return lax.dot_general(a, b, (((1,), (1,)), ((), ())), preferred_element_type=F32)


def matmul(a, b):
    return jnp.dot(a, b, preferred_element_type=F32)


def t_matmul(a, b):
    return lax.dot_general(a, b, (((0,), (0,)), ((), ())), preferred_element_type=F32)


class Scorer:
    def __init__(self, scal_ref, label_ref, place_ref):
        self.temper = jnp.exp(jnp.full((1, 128), scal_ref[0], F32))
        self.bias = scal_ref[1]
        self.labels = label_ref
        self.place = place_ref[0]
        self.columns = {}
        self.sums = None

    def side(self):
        return 1 - 2 * lax.rem(self.place, 2)

    def label_row(self, offset):
        count = self.labels.shape[0]
        at = lax.rem(self.place + offset + count, count)
        return self.labels[pl.ds(at, 1), :]

    def label_column(self, name, offset):
        if name not in self.columns:
            self.columns[name] = as_column(self.label_row(offset).astype(F32))
        return self.columns[name]

    def grads(self, image, text, weight, image_label, text_label, count_it):
        scaled = self.temper * matmul_t(image, text)
        logit = scaled + self.bias
        pos = image_label == text_label.astype(F32)
        small = jnp.exp(-jnp.abs(logit))
        share = 1.0 / (1.0 + small)
        sigmoid = jnp.where(logit >= 0, share, small * share)
        grad = weight * (sigmoid - pos.astype(F32))
        if count_it:
            signed = jnp.where(pos, -logit, logit)
            loss = weight * (jnp.maximum(signed, 0.0) + jnp.log1p(small))
            terms = (loss, grad * scaled, grad)
            self.sums = terms if self.sums is None else tuple(a + b for a, b in zip(self.sums, terms))
        return grad.astype(BF16)

    def store_sums(self, out_ref, more_ref=None):
        out_ref[...] = jnp.zeros_like(out_ref) if more_ref is None else more_ref[...]
        for at in range(3):
            out_ref[at : at + 1, :] += jnp.sum(self.sums[at], axis=0, keepdims=True)


def weight_of(packed, width):
    parts = [packed[:, width + at : width + at + 1].astype(F32) for at in (0, 32, 64)]
    return parts[0] + parts[1] + parts[2]


def text_kernel(text_ref, text_unit_ref):
    text_unit_ref[...] = normalize(text_ref[...])[0].astype(BF16)


def image_kernel(image_ref, weight_ref, text_unit_ref, image_pack_ref, both_ref):
    width = image_ref.shape[1]
    u = normalize(image_ref[...])[0].astype(BF16)
    weight = as_column(weight_ref[...])
    high = weight.astype(BF16)
    rest = weight - high.astype(F32)
    middle = rest.astype(BF16)
    low = (rest - middle.astype(F32)).astype(BF16)
    lane = lax.broadcasted_iota(jnp.int32, weight.shape, 1)
    coded = jnp.where(lane < 32, high.astype(F32), jnp.where(lane < 64, middle.astype(F32), low.astype(F32))).astype(BF16)
    image_pack_ref[:, :width] = u
    image_pack_ref[:, width:] = coded
    both_ref[:, :width] = u
    both_ref[:, width : width + 128] = coded
    both_ref[:, width + 128 :] = text_unit_ref[...]


def own_kernel(scal_ref, place_ref, label_ref, own_ref, cross_ref, image_total_ref, text_total_ref, sums_ref):
    width = cross_ref.shape[1]
    scorer = Scorer(scal_ref, label_ref, place_ref)
    u, v = own_ref[:, :width], own_ref[:, width + 128 :]
    vc = cross_ref[...]
    w = weight_of(own_ref, width)
    row = scorer.label_row(0)
    col = as_column(row.astype(F32))
    g0 = scorer.grads(u, v, w, col, row, True)
    gc = scorer.grads(u, vc, w, col, scorer.label_row(scorer.side()), True)
    image_total_ref[...] = matmul(g0, v) + matmul(gc, vc)
    text_total_ref[...] = t_matmul(g0, u)
    scorer.store_sums(sums_ref)


def early_kernel(
    scal_ref, place_ref, label_ref, own_ref, before_ref, after_ref, cross_ref,
    image_in_ref, text_in_ref, sums_in_ref,
    image_total_ref, text_total_ref, cross_g_ref, four_g_ref, sums_ref,
):
    rows, width = cross_ref.shape
    scorer = Scorer(scal_ref, label_ref, place_ref)
    side = scorer.side()
    even = side == 1
    u, v = own_ref[:, :width], own_ref[:, width + 128 :]
    ua, va = after_ref[:, :width], after_ref[:, width + 128 :]
    ub, vb = before_ref[:, :width], before_ref[:, width + 128 :]
    vc = cross_ref[...]
    w, wa, wb = weight_of(own_ref, width), weight_of(after_ref, width), weight_of(before_ref, width)
    row, row_a, row_b = scorer.label_row(0), scorer.label_row(2), scorer.label_row(-2)
    row_c = scorer.label_row(side)
    col, col_a, col_b = as_column(row.astype(F32)), as_column(row_a.astype(F32)), as_column(row_b.astype(F32))
    ga = scorer.grads(u, va, w, col, row_a, True)
    gb = scorer.grads(u, vb, w, col, row_b, True)
    gfar = scorer.grads(ub, va, wb, col_b, row_a, True)
    ux = jnp.where(even, ub, ua)
    gx = scorer.grads(ux, vc, jnp.where(even, wb, wa), jnp.where(even, col_b, col_a), row_c, True)
    ta = scorer.grads(ua, v, wa, col_a, row, False)
    tb = scorer.grads(ub, v, wb, col_b, row, False)
    image_total_ref[...] = image_in_ref[...] + matmul(ga, va) + matmul(gb, vb)
    text_total_ref[...] = text_in_ref[...] + t_matmul(ta, ua) + t_matmul(tb, ub)
    cross_g_ref[...], four_g_ref[...] = gx, gfar
    scorer.store_sums(sums_ref, sums_in_ref)


def relay_kernel(
    scal_ref, place_ref, label_ref, own_ref, after_ref, before_ref, relay_ref, early_ref,
    near_ref, far_ref, sums_ref,
):
    width = relay_ref.shape[1]
    scorer = Scorer(scal_ref, label_ref, place_ref)
    side = scorer.side()
    even = side == 1
    vr = relay_ref[...]
    row_r = scorer.label_row(-side)
    col = as_column(scorer.label_row(0).astype(F32))
    col_x = as_column(scorer.label_row(2 * side).astype(F32))
    near_ref[...] = scorer.grads(own_ref[:, :width], vr, weight_of(own_ref, width), col, row_r, True)
    ux = jnp.where(even, after_ref[:, :width], before_ref[:, :width])
    wx = jnp.where(even, weight_of(after_ref, width), weight_of(before_ref, width))
    far_ref[...] = scorer.grads(ux, vr, wx, col_x, row_r, True)
    lane = lax.broadcasted_iota(jnp.int32, (1, 128), 1)
    message = jnp.zeros((1, 128), F32)
    for at in range(3):
        total = jnp.sum(scorer.sums[at], axis=0, keepdims=True) + early_ref[at : at + 1, :]
        message = jnp.where(lane == at, jnp.sum(total, axis=1, keepdims=True), message)
    sums_ref[...] = jnp.broadcast_to(message.reshape(1, 1, 128), sums_ref.shape)


def late_kernel(
    scal_ref, place_ref, label_any, own_any, after_any, before_any, cross_any, relay_any, relay_v_any,
    far_g_any, cross_v_any, far_cross_any, four_any,
    to_up_ref, to_down_ref, cross_g_ref, relay_g_ref,
    label_ref, v_ref, va_ref, before_ref, cross_ref, relay_ref, relay_v_ref, far_g_ref, cross_v_ref, far_cross_ref, four_ref,
    sems,
):
    rows, width = relay_v_ref.shape
    text_part = (slice(None), pl.ds(width + 128, width))
    copies = [
        pltpu.make_async_copy(source, target, sems.at[at])
        for at, (source, target) in enumerate((
            (label_any, label_ref),
            (cross_any, cross_ref),
            (own_any.at[text_part], v_ref),
            (before_any, before_ref),
            (after_any.at[text_part], va_ref),
            (relay_any, relay_ref),
            (far_g_any, far_g_ref),
            (relay_v_any, relay_v_ref),
            (cross_v_any, cross_v_ref),
            (far_cross_any, far_cross_ref),
            (four_any, four_ref),
        ))
    ]
    for copy in copies:
        copy.start()
    for copy in copies[:3]:
        copy.wait()
    scorer = Scorer(scal_ref, label_ref, place_ref)
    side = scorer.side()
    even = side == 1
    v = v_ref[...]
    uc = cross_ref[:, :width]
    wc = weight_of(cross_ref, width)
    col_c = as_column(scorer.label_row(side).astype(F32))
    col_r = as_column(scorer.label_row(-side).astype(F32))
    row, row_a, row_b = scorer.label_row(0), scorer.label_row(2), scorer.label_row(-2)
    cross_g_ref[...] = scorer.grads(uc, v, wc, col_c, row, False)
    for copy in copies[3:5]:
        copy.wait()
    va, vb = va_ref[...], before_ref[:, width + 128 :]
    gcx = scorer.grads(uc, jnp.where(even, vb, va), wc, col_c, jnp.where(even, row_b, row_a), False)
    for copy in copies[5:]:
        copy.wait()
    ur, wr = relay_ref[:, :width], weight_of(relay_ref, width)
    grx = scorer.grads(ur, jnp.where(even, va, vb), wr, col_r, jnp.where(even, row_a, row_b), False)
    relay_g_ref[...] = scorer.grads(ur, v, wr, col_r, row, False)
    far_text_c, far_text_r = t_matmul(gcx, uc), t_matmul(grx, ur)
    far_image_r = matmul(far_g_ref[...], relay_v_ref[...])
    far_image_c = matmul(far_cross_ref[...], cross_v_ref[...])
    g = four_ref[...]
    to_up_ref[:rows, :] = jnp.where(even, far_image_r, far_image_c).astype(BF16)
    to_up_ref[rows:, :] = (t_matmul(g, before_ref[:, :width]) + jnp.where(even, far_text_r, far_text_c)).astype(BF16)
    to_down_ref[:rows, :] = (matmul(g, va) + jnp.where(even, far_image_c, far_image_r)).astype(BF16)
    to_down_ref[rows:, :] = jnp.where(even, far_text_c, far_text_r).astype(BF16)


def middle_kernel(got_ref, sums_ref):
    total = jnp.sum(got_ref[...], axis=0, keepdims=True)
    sums_ref[...] = jnp.broadcast_to(total.reshape(1, 1, 128), sums_ref.shape)


def final_kernel(
    count, scal_ref, image_ref, text_ref, image_total_ref, text_total_ref, near_g_ref, relay_v_ref,
    cross_g_ref, cross_ref, relay_g_ref, relay_ref, up_ref, down_ref, got_ref,
    image_grad_ref, text_grad_ref, stats_ref,
):
    rows, width = image_ref.shape
    temper = jnp.exp(jnp.full((1, 128), scal_ref[0], F32))[:, :1]
    image_more = matmul(near_g_ref[...], relay_v_ref[...])
    text_more = t_matmul(cross_g_ref[...], cross_ref[:, :width]) + t_matmul(relay_g_ref[...], relay_ref[:, :width])
    for raw_ref, total_ref, more, out_ref, at in (
        (image_ref, image_total_ref, image_more, image_grad_ref, 0),
        (text_ref, text_total_ref, text_more, text_grad_ref, rows),
    ):
        total = total_ref[...] + more + up_ref[at : at + rows, :].astype(F32) + down_ref[at : at + rows, :].astype(F32)
        unit, scale = normalize(raw_ref[...])
        out_ref[...] = norm_back(unit, scale, temper * total).astype(BF16)
    got = jnp.sum(got_ref[...], axis=0, keepdims=True) / count
    for at in range(3):
        stats_ref[at] = got[0, at]


def call(kernel, ins, outs, name, work, out_specs=None, scratch=()):
    return pl.pallas_call(
        kernel,
        out_shape=outs,
        in_specs=ins,
        out_specs=jax.tree.map(lambda _: VMEM, outs) if out_specs is None else out_specs,
        scratch_shapes=scratch,
        compiler_params=PARAMS,
        cost_estimate=pl.CostEstimate(flops=work, bytes_accessed=0, transcendentals=0),
        name=name,
    )


def exchanged(sent, axis):
    return lax.all_to_all(sent, axis, 0, 0).reshape(sent.shape[0], 128)


def per_device(images, texts, labels, weights, log_temp, bias):
    cycle = lax.axis_size("blk")
    groups = lax.axis_size("group")
    rows, width = images.shape
    place = lax.axis_index("blk").astype(jnp.int32).reshape(1)
    scal = jnp.concatenate([log_temp, bias])
    head = [SMEM, SMEM, VMEM]
    dot = 2 * rows * rows * width

    def passed(value, step_of):
        return lax.ppermute(value, "blk", [(p, (p + step_of(p)) % cycle) for p in range(cycle)])

    def across(value):
        return passed(value, lambda p: 1 - 2 * (p % 2))

    def relayed(value):
        return passed(value, lambda p: 2 - 4 * (p % 2))

    def upward(value):
        return passed(value, lambda p: 2)

    def downward(value):
        return passed(value, lambda p: -2)

    block, square = shape(rows, width, F32), shape(rows, rows, BF16)
    text_unit = call(text_kernel, [VMEM], shape(rows, width, BF16), "text", 10 * dot)(texts)
    cross_v = across(text_unit)
    image_pack, both = call(
        image_kernel,
        [VMEM] * 3,
        (shape(rows, width + 128, BF16), shape(rows, 2 * width + 128, BF16)),
        "image",
        10 * dot,
    )(images, weights.reshape(1, rows), text_unit)
    after = downward(both)
    before = upward(both)
    cross_u = across(image_pack)
    relay_v = relayed(cross_v)
    image_total, text_total, sums = call(
        own_kernel, head + [VMEM] * 2, (block,) * 2 + (shape(8, 128, F32),), "own", 150 * dot
    )(scal, place, labels, both, cross_v)
    image_total, text_total, far_cross_g, four_g, sums = call(
        early_kernel, head + [VMEM] * 7, (block, block, square, square, shape(8, 128, F32)), "early", 20 * dot
    )(scal, place, labels, both, before, after, cross_v, image_total, text_total, sums)
    near_g, far_g, sums = call(
        relay_kernel,
        head + [VMEM] * 5,
        (square, square, jax.ShapeDtypeStruct((groups, 1, 128), F32)),
        "relay", 10 * dot
    )(scal, place, labels, both, after, before, relay_v, sums)
    cross_u, sums = lax.optimization_barrier((cross_u, sums))
    relay_u = relayed(cross_u)
    got = exchanged(sums, "group")
    half, pack = pltpu.VMEM((rows, width), BF16), pltpu.VMEM((rows, width + 128), BF16)
    scratch = [pltpu.VMEM(labels.shape, jnp.int32), half, half, pltpu.VMEM(both.shape, BF16), pack, pack, half]
    block_g = pltpu.VMEM((rows, rows), BF16)
    scratch += [block_g, half, block_g, block_g]
    to_up, to_down, cross_g, relay_g = call(
        late_kernel,
        [SMEM, SMEM] + [HBM] * 11,
        (shape(2 * rows, width, BF16),) * 2 + (shape(rows, rows, BF16),) * 2,
        "late",
        400 * dot,
        scratch=scratch + [pltpu.SemaphoreType.DMA((11,))],
    )(scal, place, labels, both, after, before, cross_u, relay_u, relay_v, far_g, cross_v, far_cross_g, four_g)
    from_below = upward(to_up)
    from_above = downward(to_down)
    sums = call(middle_kernel, [VMEM], jax.ShapeDtypeStruct((cycle, 1, 128), F32), "middle", 300 * dot)(got)
    got = exchanged(sums, "blk")
    count = float(cycle * groups * rows) * float(rows) * 8.0
    image_grad, text_grad, stats = call(
        functools.partial(final_kernel, count),
        [SMEM] + [VMEM] * 13,
        (shape(rows, width, BF16),) * 2 + (jax.ShapeDtypeStruct((3,), F32),),
        "final",
        10 * dot,
        (VMEM, VMEM, SMEM),
    )(
        scal, images, texts, image_total, text_total, near_g, relay_v, cross_g, cross_u, relay_g, relay_u,
        from_below, from_above, got,
    )
    return image_grad, text_grad, stats


def solution(mesh):
    rows = P(("blk", "group"), None)
    in_specs = (rows, rows, P(None, "group"), P(("blk", "group")), P(), P())
    return jax.shard_map(per_device, mesh=mesh, in_specs=in_specs, out_specs=(rows, rows, P()), check_vma=False)
```
